32 devices in a mesh: ens: 2 (over y), node: 4 (over z), feat: 4 (over x, core).
Axes of the slice: x: 2, y: 2, z: 4, core: 2. Of those that a mesh axis runs over, the one named last changes fastest.
Arguments:
- nodes: bfloat16 [4096, 512], P(('ens', 'node', 'feat')), parts along dimension 0, may hold values from -6 to 6
- edges: bfloat16 [65536, 512], P(('ens', 'node', 'feat')), parts along dimension 0, may hold values from -6 to 6
- near_table: int32 [32, 5, 48], P(('ens', 'node', 'feat')), parts along dimension 0, may hold values from 0 to 127, as said below
- far_table: int32 [32, 16, 2], P(('ens', 'node', 'feat')), parts along dimension 0, may hold values from 0 to 127, as said below
- edge_sender: int32 [65536], P(('ens', 'node', 'feat')), parts along dimension 0, may hold values from 0 to 271, as said below
- edge_receiver: int32 [65536], P(('ens', 'node', 'feat')), parts along dimension 0, may hold values from 0 to 271, as said below
- edge_w1: bfloat16 [2, 1536, 512], replicated, may hold values from -0.15625 to 0.15625
- edge_b1: float32 [2, 512], replicated, may hold values from -4 to 4
- edge_w2: bfloat16 [2, 512, 512], replicated, may hold values from -0.25 to 0.25
- edge_gain: float32 [2, 512], replicated, may hold values from 0.5 to 1.5
- edge_shift: float32 [2, 512], replicated, may hold values from -3 to 3
- node_w1: bfloat16 [2, 1024, 512], replicated, may hold values from -0.1875 to 0.1875
- node_b1: float32 [2, 512], replicated, may hold values from -4 to 4
- node_w2: bfloat16 [2, 512, 512], replicated, may hold values from -0.25 to 0.25
- node_gain: float32 [2, 512], replicated, may hold values from 0.5 to 1.5
- node_shift: float32 [2, 512], replicated, may hold values from -3 to 3
Outputs:
- node_out: bfloat16 [4096, 512], P(('ens', 'node', 'feat')), parts along dimension 0
- edge_out: bfloat16 [65536, 512], P(('ens', 'node', 'feat')), parts along dimension 0
The draws below stay inside these ranges and needn't reach their ends.
There are 2 independent parts, one for each index of `ens`. The reference program is written for one: setup_inputs(seed, part) draws one part's arguments, and reference() takes and returns one part's arrays. A program takes and returns all parts, laid end to end along the dimension named above; an argument that names none is the same for every part. Nothing has to cross between parts.
Inputs may be any that keep to these rules, and one draw needn't show every extreme that they name: `near_table`: entry [p, k, c] is a row among the 128 nodes of device p. `far_table`: entry [p, q, c] is a row among the 128 nodes of device p. `edge_sender`: an edge's entry names a near slot (below (5) * 48) or a far slot of the tables as the steps read them. `edge_receiver`: an edge's entry names a near slot (below (5) * 48) or a far slot of the tables as the steps read them.
All inputs are finite; a program needn't handle non-finite values.
Results may differ from the reference program's by a relative error of at most 0.012.
Values may be sent and summed in bfloat16 or wider, within the bound.
A program may use at most 64 MiB of HBM per device.

```python
import jax
import jax.numpy as jnp
from jax import lax

D = 512
NODE_DEV = 128
EDGE_DEV = 2048
REACH = 2
NEAR = 48
CAP = 2
LAYERS = 2
PEERS = 16
NODES = 2048
EDGES = 32768


def endpoint_slots(key, salt_value, far_phase, low_position, high_position):
    total = PEERS * EDGE_DEV
    near_rows = (2 * REACH + 1) * NEAR
    position = jnp.arange(total, dtype=jnp.int32) % EDGE_DEV
    offsets = jnp.array([0, 0, 0, 0, -1, 1, -1, 1, -2, 2], dtype=jnp.int32)
    picked = jax.random.randint(jax.random.fold_in(key, salt_value + 1), (total,), 0, 10)
    offset_index = jnp.clip(offsets[picked], -REACH, REACH) + REACH
    near_slot = offset_index * NEAR + jax.random.randint(jax.random.fold_in(key, salt_value + 2), (total,), 0, NEAR)
    far_slot = near_rows + jax.random.randint(jax.random.fold_in(key, salt_value + 3), (total,), 0, PEERS * CAP)
    slots = jnp.where(position % 8 == far_phase, far_slot, near_slot)
    slots = jnp.where(position == low_position, 0, slots)
    slots = jnp.where(position == high_position, near_rows + PEERS * CAP - 1, slots)
    return slots.astype(jnp.int32)


def draw_near_table(key, part):
    picked = jax.random.randint(jax.random.fold_in(key, 5), (PEERS, 2 * REACH + 1, NEAR), 0, NODE_DEV)
    picked = picked.at[0, 0, 0].set(0)
    picked = picked.at[PEERS - 1, 2 * REACH, NEAR - 1].set(NODE_DEV - 1)
    return picked.astype(jnp.int32)


def draw_far_table(key, part):
    picked = jax.random.randint(jax.random.fold_in(key, 7), (PEERS, PEERS, CAP), 0, NODE_DEV)
    picked = picked.at[0, 0, 0].set(0)
    picked = picked.at[PEERS - 1, PEERS - 1, CAP - 1].set(NODE_DEV - 1)
    return picked.astype(jnp.int32)


def draw_edge_sender(key, part):
    return endpoint_slots(key, 20, 0, 1, EDGE_DEV - 1)


def draw_edge_receiver(key, part):
    return endpoint_slots(key, 40, 4, 2, EDGE_DEV - 2)


def level_of(key, extent, split, low, largest):
    factor_of, own = 1.0, jax.random.fold_in(key, 6)
    for dim, parts in split:
        steps = jnp.exp(jax.random.uniform(jax.random.fold_in(own, dim), (parts,), jnp.float32, low / len(split), largest / len(split)))
        factor_of = factor_of * jnp.repeat(steps, extent[dim] // parts).reshape([-1 if axis == dim else 1 for axis in range(len(extent))])
    return factor_of


def noise(own_key, dims, width, limit, shards=(), held_as=jnp.bfloat16):
    result = width * jax.random.normal(own_key, dims, jnp.float32)
    if shards:
        result = result * level_of(own_key, dims, shards, -0.22, 0.18)
    return jnp.clip(result, -limit, limit).astype(held_as)


def setup_inputs(seed: int = 0, part: int = 0) -> dict:
    seeds = jax.random.split(jax.random.key(seed), 17)
    own_keys = jax.random.split(jax.random.fold_in(seeds[16], part), 17)
    nodes = noise(own_keys[0], (NODES, D), 1.0, 6.0, ((0, 16),))
    edges = noise(own_keys[1], (EDGES, D), 1.0, 6.0, ((0, 16),))
    near_table = draw_near_table(jax.random.fold_in(jax.random.fold_in(seeds[16], part), 71), part)
    far_table = draw_far_table(jax.random.fold_in(jax.random.fold_in(seeds[16], part), 71), part)
    edge_sender = draw_edge_sender(jax.random.fold_in(jax.random.fold_in(seeds[16], part), 71), part)
    edge_receiver = draw_edge_receiver(jax.random.fold_in(jax.random.fold_in(seeds[16], part), 71), part)
    edge_w1 = noise(seeds[6], (LAYERS, 3 * D, D), (3 * D) ** -0.5, 0.15625)
    edge_b1 = noise(seeds[7], (LAYERS, D), 1.0, 4.0, (), jnp.float32)
    edge_w2 = noise(seeds[8], (LAYERS, D, D), D ** -0.5, 0.25)
    edge_gain = jnp.clip(jax.random.uniform(seeds[9], (LAYERS, D), jnp.float32, 0.5, 1.5), 0.5, 1.5)
    edge_shift = noise(seeds[10], (LAYERS, D), 0.5, 3.0, (), jnp.float32)
    node_w1 = noise(seeds[11], (LAYERS, 2 * D, D), (2 * D) ** -0.5, 0.1875)
    node_b1 = noise(seeds[12], (LAYERS, D), 1.0, 4.0, (), jnp.float32)
    node_w2 = noise(seeds[13], (LAYERS, D, D), D ** -0.5, 0.25)
    node_gain = jnp.clip(jax.random.uniform(seeds[14], (LAYERS, D), jnp.float32, 0.5, 1.5), 0.5, 1.5)
    node_shift = noise(seeds[15], (LAYERS, D), 0.5, 3.0, (), jnp.float32)
    return {"nodes": nodes, "edges": edges, "near_table": near_table, "far_table": far_table, "edge_sender": edge_sender, "edge_receiver": edge_receiver, "edge_w1": edge_w1, "edge_b1": edge_b1, "edge_w2": edge_w2, "edge_gain": edge_gain, "edge_shift": edge_shift, "node_w1": node_w1, "node_b1": node_b1, "node_w2": node_w2, "node_gain": node_gain, "node_shift": node_shift}


EPSILON = 1e-05

def layer_norm(values, norm_gain, norm_shift):
    center = values - lax.optimization_barrier(jnp.mean(values, axis=-1, keepdims=True))
    spread = lax.optimization_barrier(jnp.mean(center * center, axis=-1, keepdims=True))
    return center * lax.rsqrt(spread + EPSILON) * norm_gain + norm_shift

def finish(old_state, mixed_rows, norm_gain, norm_shift):
    return (old_state.astype(jnp.float32) + layer_norm(mixed_rows, norm_gain, norm_shift)).astype(jnp.bfloat16)

def two_layer(joined, first_weight, bias_row, second_weight):
    pre_act = jnp.dot(joined, first_weight, preferred_element_type=jnp.float32)
    hidden = jax.nn.silu(pre_act + bias_row).astype(jnp.bfloat16)
    return jnp.dot(hidden, second_weight, preferred_element_type=jnp.float32)

def reference(nodes, edges, near_table, far_table, edge_sender, edge_receiver, edge_w1, edge_b1, edge_w2, edge_gain, edge_shift, node_w1, node_b1, node_w2, node_gain, node_shift):
    holder = (jnp.arange(EDGES, dtype=jnp.int32) // EDGE_DEV).astype(jnp.int32)
    near_rows = (2 * REACH + 1) * NEAR

    def global_ids(slots):
        is_near = slots < near_rows
        offset_index = jnp.minimum(slots // NEAR, 2 * REACH).astype(jnp.int32)
        near_slot = (slots % NEAR).astype(jnp.int32)
        near_source = ((holder - (offset_index - REACH)) % PEERS).astype(jnp.int32)
        near_ids = near_source * NODE_DEV + near_table[near_source, offset_index, near_slot]
        far_index = jnp.maximum(slots - near_rows, 0).astype(jnp.int32)
        far_source = (far_index // CAP).astype(jnp.int32)
        far_slot = (far_index % CAP).astype(jnp.int32)
        far_ids = far_source * NODE_DEV + far_table[far_source, holder, far_slot]
        return jnp.where(is_near, near_ids, far_ids).astype(jnp.int32)
    sender_ids = global_ids(edge_sender)
    receiver_ids = global_ids(edge_receiver)
    states = nodes
    edge_state = edges
    for layer_index in range(LAYERS):

        def update_block(packed):
            block_edges, block_send, block_recv = packed
            joined = jnp.concatenate([block_edges, states[block_send], states[block_recv]], axis=1)
            mixed_rows = two_layer(joined, edge_w1[layer_index], edge_b1[layer_index], edge_w2[layer_index])
            return finish(block_edges, mixed_rows, edge_gain[layer_index], edge_shift[layer_index])
        edge_state = lax.map(update_block, (edge_state.reshape(PEERS, EDGE_DEV, D), sender_ids.reshape(PEERS, EDGE_DEV), receiver_ids.reshape(PEERS, EDGE_DEV))).reshape(EDGES, D)
        aggregate = jax.ops.segment_sum(edge_state.astype(jnp.float32), receiver_ids, num_segments=NODES)
        joined_nodes = jnp.concatenate([states, aggregate.astype(jnp.bfloat16)], axis=1)
        node_mixed = two_layer(joined_nodes, node_w1[layer_index], node_b1[layer_index], node_w2[layer_index])
        states = finish(states, node_mixed, node_gain[layer_index], node_shift[layer_index])
    return (states, edge_state)
```

```python
import functools

import jax
import jax.numpy as jnp
from jax import lax
from jax.experimental import pallas as pl
from jax.experimental.pallas import tpu as pltpu
from jax.sharding import PartitionSpec as P

EPSILON = 1e-05
LANES = 128
BLOCK = 256
AXES = ("ens", "node", "feat")
MESH = pl.DeviceIdType.MESH


def round_up(value, multiple):
    return -(-value // multiple) * multiple


def dot(a, b):
    return jnp.dot(a, b, preferred_element_type=jnp.float32)


def layer_norm(values, norm_gain, norm_shift):
    center = values - jnp.mean(values, axis=-1, keepdims=True)
    spread = jnp.mean(center * center, axis=-1, keepdims=True)
    return center * lax.rsqrt(spread + EPSILON) * norm_gain + norm_shift


def gated(half):
    return (half + half * jnp.tanh(half)).astype(jnp.bfloat16)


def kernel(
    sizes,
    nodes, owner, senders, receivers,
    edge_b1, edge_gain, edge_shift, node_b1, node_gain, node_shift,
    edges_hbm, edge_w1_hbm, edge_w2_hbm, node_w1_hbm, node_w2_hbm,
    node_out, edge_out,
    edge_w1, edge_w2, node_w1, node_w2,
    states, edges, partial, hot, hot_t, owner_t, projected, sums,
    near_out, near_in, near_back_out, near_back_in,
    far_out, far_in, far_back_out, far_back_in,
    load_sems, store_sems,
    near_send, near_recv, far_send, far_recv,
):
    peers, feat_size, layers, span, near_width, cap, slots = sizes
    reach = (span - 1) // 2
    near_total = span * near_width
    padded = owner_t.shape[1]
    features = states.shape[1]
    columns = features // LANES
    edge_count = edges.shape[0]
    blocks = edge_count // BLOCK
    ens = lax.axis_index("ens")
    me = lax.axis_index("node") * feat_size + lax.axis_index("feat")

    def device(index):
        return (ens, index // feat_size, index % feat_size)

    loads = [pltpu.make_async_copy(edges_hbm, edges, load_sems.at[0])]
    for layer in range(layers):
        for place, (source, target) in enumerate(
            ((edge_w1_hbm, edge_w1), (edge_w2_hbm, edge_w2), (node_w1_hbm, node_w1), (node_w2_hbm, node_w2))
        ):
            loads.append(
                pltpu.make_async_copy(source.at[layer], target.at[layer], load_sems.at[1 + 4 * layer + place])
            )
    for load in loads:
        load.start()

    barrier = pltpu.get_barrier_semaphore()

    def greet(step, carry):
        pl.semaphore_signal(barrier, inc=1, device_id=device((me + step) % peers), device_id_type=MESH)
        return carry

    lax.fori_loop(1, peers, greet, 0)

    node_rows = states.shape[0]
    row_ids = lax.broadcasted_iota(jnp.int32, (node_rows, LANES), 0)
    for j in range(padded // LANES):
        picked = owner[:, j * LANES : (j + 1) * LANES] == row_ids
        owner_t[:, j * LANES : (j + 1) * LANES] = jnp.where(picked, 1.0, 0.0)

    states[...] = nodes[...]

    def near_copy(way, layer, k):
        source, target = ((near_out, near_in), (near_back_out, near_back_in))[way]
        rows = pl.ds(k * near_width, near_width)
        shift = (k - reach) if way == 0 else (reach - k)
        slot = (way * layers + layer) * span + k
        return pltpu.make_async_remote_copy(
            src_ref=source.at[layer, rows],
            dst_ref=target.at[layer, rows],
            send_sem=near_send.at[slot],
            recv_sem=near_recv.at[slot],
            device_id=device((me + shift + peers) % peers),
            device_id_type=MESH,
        )

    def far_copy(way, layer, step):
        source, target = ((far_out, far_in), (far_back_out, far_back_in))[way]
        to = (me + step) % peers
        slot = (way * layers + layer) * peers + step
        return pltpu.make_async_remote_copy(
            src_ref=source.at[layer, to],
            dst_ref=target.at[layer, me],
            send_sem=far_send.at[slot],
            recv_sem=far_recv.at[slot],
            device_id=device(to),
            device_id_type=MESH,
        )

    def far_arrival(way, layer, step):
        source, target = ((far_out, far_in), (far_back_out, far_back_in))[way]
        origin = (me + peers - step) % peers
        slot = (way * layers + layer) * peers + step
        return pltpu.make_async_remote_copy(
            src_ref=source.at[layer, origin],
            dst_ref=target.at[layer, origin],
            send_sem=far_send.at[slot],
            recv_sem=far_recv.at[slot],
            device_id=device(origin),
            device_id_type=MESH,
        )

    def send(way, layer, rows, first=False):
        source, far_source = ((near_out, far_out), (near_back_out, far_back_out))[way]
        target, far_target = ((near_in, far_in), (near_back_in, far_back_in))[way]
        source[layer, :near_total, :] = rows[:near_total].astype(jnp.bfloat16)
        for s in range(cap):
            begin = near_total + s * peers
            for c in range(columns):
                far_source[layer, :, s * columns + c, :] = rows[begin : begin + peers, c * LANES : (c + 1) * LANES]
        if first:
            pl.semaphore_wait(barrier, peers - 1)
        for k in range(span):
            if k != reach:
                near_copy(way, layer, k).start()

        def start(step, carry):
            far_copy(way, layer, step).start()
            return carry

        lax.fori_loop(1, peers, start, 0)
        own = slice(reach * near_width, (reach + 1) * near_width)
        target[layer, own, :] = source[layer, own, :]
        far_target[layer, pl.ds(me, 1)] = far_source[layer, pl.ds(me, 1)]
        target[layer, slots:, :] = jnp.zeros((padded - slots, features), jnp.bfloat16)

    def receive(way, layer):
        target, far_target = ((near_in, far_in), (near_back_in, far_back_in))[way]
        for k in range(span):
            if k != reach:
                near_copy(way, layer, k).wait_recv()

        def wait(step, carry):
            far_arrival(way, layer, step).wait_recv()
            return carry

        lax.fori_loop(1, peers, wait, 0)
        for s in range(cap):
            begin = near_total + s * peers
            for c in range(columns):
                target[layer, begin : begin + peers, c * LANES : (c + 1) * LANES] = far_target[
                    layer, :, s * columns + c, :
                ].astype(jnp.bfloat16)

    def gathered():
        pick = jnp.transpose(owner_t[...]).astype(jnp.bfloat16)
        return dot(pick, states[...])

    send(0, 0, gathered(), first=True)

    def renumbered(index):
        value = index.astype(jnp.float32)
        far = value - near_total
        peer = jnp.floor((far + 0.5) * (1.0 / cap))
        return jnp.where(value < near_total, value, near_total + (far - peer * cap) * peers + peer)

    sender_ids = renumbered(senders[...])
    receiver_ids = renumbered(receivers[...])
    lane_ids = lax.broadcasted_iota(jnp.int32, (LANES, LANES), 1).astype(jnp.float32)
    slot_ids = lax.broadcasted_iota(jnp.int32, (hot_t.shape[1], LANES), 0).astype(jnp.float32)
    for b in range(edge_count // LANES):
        rows = slice(b * LANES, (b + 1) * LANES)
        for side, ids in enumerate((sender_ids, receiver_ids)):
            column = jnp.transpose(jnp.broadcast_to(ids[b : b + 1], (LANES, LANES)))
            for j in range(padded // LANES):
                begin = side * padded + j * LANES
                hot[rows, begin : begin + LANES] = jnp.where(column == lane_ids + j * LANES, 1.0, 0.0).astype(
                    jnp.bfloat16
                )
        begin = (b * LANES) % BLOCK
        hot_t[b * LANES // BLOCK, :, begin : begin + LANES] = jnp.where(
            receiver_ids[b : b + 1] == slot_ids, 1.0, 0.0
        ).astype(jnp.bfloat16)

    loads[0].wait()
    for layer in range(layers):
        for place in range(4):
            if layer == 0 and place == 0:
                loads[1].wait()

        def own_term(i, carry, layer=layer):
            rows = pl.ds(pl.multiple_of(i * BLOCK, BLOCK), BLOCK)
            partial[rows, :] = 0.5 * (
                dot(edges[rows, :], edge_w1[layer, :features, :]) + edge_b1[layer : layer + 1, :]
            )
            return carry

        if layer == 0:
            lax.fori_loop(0, blocks, own_term, 0)
            for load in loads[2:]:
                load.wait()

        receive(0, layer)
        arrived = near_in[layer]
        for side in range(2):
            begin = (1 + side) * features
            projected[side * padded : (side + 1) * padded, :] = (
                0.5 * dot(arrived, edge_w1[layer, begin : begin + features, :])
            ).astype(jnp.bfloat16)

        sums[...] = jnp.zeros_like(sums)

        def update(i, carry, layer=layer):
            rows = pl.ds(pl.multiple_of(i * BLOCK, BLOCK), BLOCK)
            half = partial[rows, :] + dot(hot[rows, :], projected[...])
            mixed = dot(gated(half), edge_w2[layer])
            fresh = edges[rows, :].astype(jnp.float32) + layer_norm(
                mixed, edge_gain[layer : layer + 1, :], edge_shift[layer : layer + 1, :]
            )
            fresh = fresh.astype(jnp.bfloat16)
            edges[rows, :] = fresh
            if layer == layers - 1:
                pltpu.make_async_copy(edges.at[rows], edge_out.at[rows], store_sems.at[i]).start()
            sums[...] += dot(hot_t[i], fresh)
            return carry

        lax.fori_loop(0, blocks, update, 0)

        send(1, layer, sums)
        pre = dot(states[...], node_w1[layer, :features, :]) + node_b1[layer : layer + 1, :]
        if layer + 1 < layers:
            lax.fori_loop(0, blocks, functools.partial(own_term, layer=layer + 1), 0)
        receive(1, layer)
        aggregate = dot(owner_t[...].astype(jnp.bfloat16), near_back_in[layer]).astype(jnp.bfloat16)
        half = 0.5 * (pre + dot(aggregate, node_w1[layer, features:, :]))
        mixed = dot(gated(half), node_w2[layer])
        fresh = states[...].astype(jnp.float32) + layer_norm(
            mixed, node_gain[layer : layer + 1, :], node_shift[layer : layer + 1, :]
        )
        states[...] = fresh.astype(jnp.bfloat16)
        if layer + 1 < layers:
            send(0, layer + 1, gathered())

    node_out[...] = states[...]

    def drain(i, carry):
        rows = pl.ds(pl.multiple_of(i * BLOCK, BLOCK), BLOCK)
        pltpu.make_async_copy(edges.at[rows], edge_out.at[rows], store_sems.at[i]).wait()
        return carry

    lax.fori_loop(0, blocks, drain, 0)
    for way in range(2):
        for layer in range(layers):
            for k in range(span):
                if k != reach:
                    near_copy(way, layer, k).wait_send()

            def sent(step, carry, way=way, layer=layer):
                far_copy(way, layer, step).wait_send()
                return carry

            lax.fori_loop(1, peers, sent, 0)


def on_device(
    nodes,
    edges,
    near_table,
    far_table,
    edge_sender,
    edge_receiver,
    edge_w1,
    edge_b1,
    edge_w2,
    edge_gain,
    edge_shift,
    node_w1,
    node_b1,
    node_w2,
    node_gain,
    node_shift,
):
    peers = lax.axis_size(("node", "feat"))
    feat_size = lax.axis_size("feat")
    span, near_width = near_table.shape[1:]
    cap = far_table.shape[2]
    near_total = span * near_width
    slots = near_total + peers * cap
    padded = round_up(slots + 1, LANES)
    node_rows, features = nodes.shape
    edge_count = edges.shape[0]
    layers = edge_w1.shape[0]
    blocks = edge_count // BLOCK
    owner = jnp.concatenate(
        [near_table.reshape(1, near_total), far_table.reshape(peers, cap).T.reshape(1, peers * cap)], axis=1
    )
    owner = jnp.pad(owner, ((0, 0), (0, padded - slots)), constant_values=-1)
    senders = edge_sender.reshape(edge_count // LANES, LANES)
    receivers = edge_receiver.reshape(edge_count // LANES, LANES)
    tile = cap * features // LANES
    bf16, f32 = jnp.bfloat16, jnp.float32
    sizes = (peers, feat_size, layers, span, near_width, cap, slots)
    vmem = pl.BlockSpec(memory_space=pltpu.VMEM)
    hbm = pl.BlockSpec(memory_space=pl.ANY)
    near_buffer = pltpu.VMEM((layers, padded, features), bf16)
    far_buffer = pltpu.VMEM((layers, peers, tile, LANES), f32)
    flops = 2 * layers * edge_count * features * (2 * features + 2 * padded + slots)
    return pl.pallas_call(
        functools.partial(kernel, sizes),
        out_shape=(
            jax.ShapeDtypeStruct(nodes.shape, bf16),
            jax.ShapeDtypeStruct(edges.shape, bf16),
        ),
        in_specs=[vmem] * 10 + [hbm] * 5,
        out_specs=(vmem, hbm),
        scratch_shapes=[
            pltpu.VMEM(edge_w1.shape, bf16),
            pltpu.VMEM(edge_w2.shape, bf16),
            pltpu.VMEM(node_w1.shape, bf16),
            pltpu.VMEM(node_w2.shape, bf16),
            pltpu.VMEM(nodes.shape, bf16),
            pltpu.VMEM(edges.shape, bf16),
            pltpu.VMEM(edges.shape, f32),
            pltpu.VMEM((edge_count, 2 * padded), bf16),
            pltpu.VMEM((blocks, round_up(slots, 16), BLOCK), bf16),
            pltpu.VMEM((node_rows, padded), f32),
            pltpu.VMEM((2 * padded, features), bf16),
            pltpu.VMEM((round_up(slots, 16), features), f32),
            near_buffer, near_buffer, near_buffer, near_buffer,
            far_buffer, far_buffer, far_buffer, far_buffer,
            pltpu.SemaphoreType.DMA((1 + 4 * layers,)),
            pltpu.SemaphoreType.DMA((blocks,)),
            pltpu.SemaphoreType.DMA((2 * layers * span,)),
            pltpu.SemaphoreType.DMA((2 * layers * span,)),
            pltpu.SemaphoreType.DMA((2 * layers * peers,)),
            pltpu.SemaphoreType.DMA((2 * layers * peers,)),
        ],
        compiler_params=pltpu.CompilerParams(
            collective_id=0, has_side_effects=True, vmem_limit_bytes=50 * 2**20
        ),
        cost_estimate=pl.CostEstimate(flops=flops, bytes_accessed=12 * 2**20, transcendentals=0),
    )(
        nodes, owner, senders, receivers,
        edge_b1, edge_gain, edge_shift, node_b1, node_gain, node_shift,
        edges, edge_w1, edge_w2, node_w1, node_w2,
    )


def solution(mesh):
    split = P(AXES, None)
    table = P(AXES, None, None)
    return jax.shard_map(
        on_device,
        mesh=mesh,
        in_specs=(split, split, table, table, P(AXES), P(AXES)) + (P(),) * 10,
        out_specs=(split, split),
        check_vma=False,
    )
```

```python
import functools

import jax
import jax.numpy as jnp
from jax import lax
from jax.experimental import pallas as pl
from jax.experimental.pallas import tpu as pltpu
from jax.sharding import PartitionSpec as P

EPSILON = 1e-05
LANES = 128
BLOCK = 256
AXES = ("ens", "node", "feat")
MESH = pl.DeviceIdType.MESH


def round_up(value, multiple):
    return -(-value // multiple) * multiple


def dot(a, b):
    return jnp.dot(a, b, preferred_element_type=jnp.float32)


def layer_norm(center, norm_gain, norm_shift):
    spread = jnp.mean(center * center, axis=-1, keepdims=True)
    return center * lax.rsqrt(spread + EPSILON) * norm_gain + norm_shift


def gated(half):
    return (half + half * jnp.tanh(half)).astype(jnp.bfloat16)


def kernel(
    sizes,
    nodes_hbm, near_hbm, far_hbm, senders_hbm, receivers_hbm,
    edge_b1_hbm, edge_gain_hbm, edge_shift_hbm, node_b1_hbm, node_gain_hbm, node_shift_hbm,
    edges_hbm, edge_w1_hbm, edge_w2_hbm, node_w1_hbm, node_w2_hbm,
    states, edge_out,
    edges,
    near_table, far_table, senders, receivers,
    edge_b1, edge_gain, edge_shift, node_b1, node_gain, node_shift,
    edge_w1, edge_w2, node_w1, node_w2,
    partial, hidden_even, hidden_odd, hot, hot_t, pick, projected, sums,
    near_out, near_in, near_back_out, near_back_in,
    far_out, far_in, far_back_out, far_back_in,
    load_sems, store_sems,
    near_send, near_recv, far_send, far_recv,
):
    peers, feat_size, layers, span, near_width, cap, slots = sizes
    reach = (span - 1) // 2
    near_total = span * near_width
    padded = pick.shape[0]
    features = states.shape[1]
    columns = features // LANES
    edge_count = edges.shape[0]
    blocks = edge_count // BLOCK
    ens = lax.axis_index("ens")
    me = lax.axis_index("node") * feat_size + lax.axis_index("feat")

    def device(index):
        return (ens, index // feat_size, index % feat_size)

    loads = []

    def load(source, target):
        copy = pltpu.make_async_copy(source, target, load_sems.at[len(loads)])
        copy.start()
        loads.append(copy)
        return copy

    first_loads = [load(nodes_hbm, states), load(near_hbm, near_table), load(far_hbm, far_table)]
    index_loads = [load(senders_hbm, senders), load(receivers_hbm, receivers)]
    own_loads = [load(edge_b1_hbm, edge_b1), load(edges_hbm, edges), load(edge_w1_hbm.at[0], edge_w1.at[0])]
    late_loads = [
        load(edge_gain_hbm, edge_gain),
        load(edge_shift_hbm, edge_shift),
        load(node_b1_hbm, node_b1),
        load(node_gain_hbm, node_gain),
        load(node_shift_hbm, node_shift),
        load(edge_w2_hbm, edge_w2),
        load(node_w1_hbm, node_w1),
        load(node_w2_hbm, node_w2),
    ]
    late_loads += [load(edge_w1_hbm.at[layer], edge_w1.at[layer]) for layer in range(1, layers)]

    barrier = pltpu.get_barrier_semaphore()

    def greet(step, carry):
        pl.semaphore_signal(barrier, inc=1, device_id=device((me + step) % peers), device_id_type=MESH)
        return carry

    lax.fori_loop(1, peers, greet, 0)

    for copy in first_loads:
        copy.wait()
    node_rows = states.shape[0]
    near_ids = lax.broadcasted_iota(jnp.int32, (near_width, node_rows), 1).astype(jnp.float32)
    far_ids = lax.broadcasted_iota(jnp.int32, (peers, node_rows), 1).astype(jnp.float32)
    for k in range(span):
        row = near_table[k].astype(jnp.float32)
        column = jnp.transpose(jnp.broadcast_to(row, (node_rows, near_width)))
        pick[k * near_width : (k + 1) * near_width, :] = jnp.where(column == near_ids, 1.0, 0.0)
    for s in range(cap):
        begin = near_total + s * peers
        row = far_table[s : s + 1, :].astype(jnp.float32)
        column = jnp.transpose(jnp.broadcast_to(row, (node_rows, peers)))
        pick[begin : begin + peers, :] = jnp.where(column == far_ids, 1.0, 0.0)
    pick[slots:, :] = jnp.zeros((padded - slots, node_rows), jnp.float32)

    def near_copy(way, layer, k):
        source, target = ((near_out, near_in), (near_back_out, near_back_in))[way]
        rows = pl.ds(k * near_width, near_width)
        shift = (k - reach) if way == 0 else (reach - k)
        slot = (way * layers + layer) * span + k
        return pltpu.make_async_remote_copy(
            src_ref=source.at[layer, rows],
            dst_ref=target.at[layer, rows],
            send_sem=near_send.at[slot],
            recv_sem=near_recv.at[slot],
            device_id=device((me + shift + peers) % peers),
            device_id_type=MESH,
        )

    def far_copy(way, layer, step):
        source, target = ((far_out, far_in), (far_back_out, far_back_in))[way]
        to = (me + step) % peers
        slot = (way * layers + layer) * peers + step
        return pltpu.make_async_remote_copy(
            src_ref=source.at[layer, to],
            dst_ref=target.at[layer, me],
            send_sem=far_send.at[slot],
            recv_sem=far_recv.at[slot],
            device_id=device(to),
            device_id_type=MESH,
        )

    def far_arrival(way, layer, step):
        source, target = ((far_out, far_in), (far_back_out, far_back_in))[way]
        origin = (me + peers - step) % peers
        slot = (way * layers + layer) * peers + step
        return pltpu.make_async_remote_copy(
            src_ref=source.at[layer, origin],
            dst_ref=target.at[layer, origin],
            send_sem=far_send.at[slot],
            recv_sem=far_recv.at[slot],
            device_id=device(origin),
            device_id_type=MESH,
        )

    def send(way, layer, rows, first=False):
        source, far_source = ((near_out, far_out), (near_back_out, far_back_out))[way]
        target, far_target = ((near_in, far_in), (near_back_in, far_back_in))[way]
        source[layer, :near_total, :] = rows[:near_total].astype(jnp.bfloat16)
        for s in range(cap):
            begin = near_total + s * peers
            for c in range(columns):
                far_source[layer, :, s * columns + c, :] = rows[begin : begin + peers, c * LANES : (c + 1) * LANES]
        if first:
            pl.semaphore_wait(barrier, peers - 1)
        for k in range(span):
            if k != reach:
                near_copy(way, layer, k).start()

        def start(step, carry):
            far_copy(way, layer, step).start()
            return carry

        lax.fori_loop(1, peers, start, 0)
        own = slice(reach * near_width, (reach + 1) * near_width)
        target[layer, own, :] = source[layer, own, :]
        far_target[layer, pl.ds(me, 1)] = far_source[layer, pl.ds(me, 1)]
        target[layer, slots:, :] = jnp.zeros((padded - slots, features), jnp.bfloat16)

    def receive(way, layer):
        target, far_target = ((near_in, far_in), (near_back_in, far_back_in))[way]
        for k in range(span):
            if k != reach:
                near_copy(way, layer, k).wait_recv()

        def wait(step, carry):
            far_arrival(way, layer, step).wait_recv()
            return carry

        lax.fori_loop(1, peers, wait, 0)
        for s in range(cap):
            begin = near_total + s * peers
            for c in range(columns):
                target[layer, begin : begin + peers, c * LANES : (c + 1) * LANES] = far_target[
                    layer, :, s * columns + c, :
                ].astype(jnp.bfloat16)

    def gathered():
        return dot(pick[...].astype(jnp.bfloat16), states[...])

    def store(i):
        rows = pl.ds(pl.multiple_of(i * BLOCK, BLOCK), BLOCK)
        return pltpu.make_async_copy(edges.at[rows], edge_out.at[rows], store_sems.at[i])

    send(0, 0, gathered(), first=True)

    def renumbered(index):
        value = index.astype(jnp.float32)
        far = value - near_total
        peer = jnp.floor((far + 0.5) * (1.0 / cap))
        return jnp.where(value < near_total, value, near_total + (far - peer * cap) * peers + peer)

    for copy in index_loads:
        copy.wait()
    sender_ids = renumbered(senders[...])
    receiver_ids = renumbered(receivers[...])
    lane_ids = lax.broadcasted_iota(jnp.int32, (LANES, LANES), 1).astype(jnp.float32)
    slot_ids = lax.broadcasted_iota(jnp.int32, (hot_t.shape[1], LANES), 0).astype(jnp.float32)
    for b in range(edge_count // LANES):
        rows = slice(b * LANES, (b + 1) * LANES)
        for side, ids in enumerate((sender_ids, receiver_ids)):
            column = jnp.transpose(jnp.broadcast_to(ids[b : b + 1], (LANES, LANES)))
            for j in range(padded // LANES):
                begin = side * padded + j * LANES
                hot[rows, begin : begin + LANES] = jnp.where(column == lane_ids + j * LANES, 1.0, 0.0).astype(
                    jnp.bfloat16
                )
        begin = (b * LANES) % BLOCK
        hot_t[b * LANES // BLOCK, :, begin : begin + LANES] = jnp.where(
            receiver_ids[b : b + 1] == slot_ids, 1.0, 0.0
        ).astype(jnp.bfloat16)

    for copy in own_loads:
        copy.wait()
    for layer in range(layers):

        def own_term(i, carry, layer=layer):
            rows = pl.ds(pl.multiple_of(i * BLOCK, BLOCK), BLOCK)
            partial[rows, :] = 0.5 * (
                dot(edges[rows, :], edge_w1[layer, :features, :]) + edge_b1[layer : layer + 1, :]
            )
            return carry

        if layer == 0:
            lax.fori_loop(0, blocks, own_term, 0)
            for copy in late_loads:
                copy.wait()
            for weight in (edge_w2, node_w2):
                for place in range(layers):
                    values = weight[place].astype(jnp.float32)
                    weight[place] = (values - jnp.mean(values, axis=-1, keepdims=True)).astype(jnp.bfloat16)

        receive(0, layer)
        arrived = near_in[layer]
        for side in range(2):
            begin = (1 + side) * features
            projected[side * padded : (side + 1) * padded, :] = (
                0.5 * dot(arrived, edge_w1[layer, begin : begin + features, :])
            ).astype(jnp.bfloat16)

        sums[...] = jnp.zeros_like(sums)

        def block_rows(i):
            return pl.ds(pl.multiple_of(i * BLOCK, BLOCK), BLOCK)

        def first_half(i, hidden):
            rows = block_rows(i)
            hidden[...] = gated(partial[rows, :] + dot(hot[rows, :], projected[...]))

        def second_half(i, hidden, layer=layer):
            rows = block_rows(i)
            mixed = dot(hidden[...], edge_w2[layer])
            fresh = edges[rows, :].astype(jnp.float32) + layer_norm(
                mixed, edge_gain[layer : layer + 1, :], edge_shift[layer : layer + 1, :]
            )
            fresh = fresh.astype(jnp.bfloat16)
            edges[rows, :] = fresh
            if layer == layers - 1:
                store(i).start()
            sums[...] += dot(hot_t[i], fresh)

        first_half(0, hidden_even)

        def update(j, carry):
            first_half(2 * j + 1, hidden_odd)
            second_half(2 * j, hidden_even)
            first_half(2 * j + 2, hidden_even)
            second_half(2 * j + 1, hidden_odd)
            return carry

        lax.fori_loop(0, blocks // 2 - 1, update, 0)
        first_half(blocks - 1, hidden_odd)
        second_half(blocks - 2, hidden_even)
        second_half(blocks - 1, hidden_odd)

        send(1, layer, sums)
        pre = dot(states[...], node_w1[layer, :features, :]) + node_b1[layer : layer + 1, :]
        if layer + 1 < layers:
            lax.fori_loop(0, blocks, functools.partial(own_term, layer=layer + 1), 0)
        receive(1, layer)
        aggregate = dot(jnp.transpose(pick[...]).astype(jnp.bfloat16), near_back_in[layer]).astype(jnp.bfloat16)
        half = 0.5 * (pre + dot(aggregate, node_w1[layer, features:, :]))
        mixed = dot(gated(half), node_w2[layer])
        fresh = states[...].astype(jnp.float32) + layer_norm(
            mixed, node_gain[layer : layer + 1, :], node_shift[layer : layer + 1, :]
        )
        states[...] = fresh.astype(jnp.bfloat16)
        if layer + 1 < layers:
            send(0, layer + 1, gathered())

    def drain(i, carry):
        store(i).wait()
        return carry

    lax.fori_loop(0, blocks, drain, 0)
    for way in range(2):
        for layer in range(layers):
            for k in range(span):
                if k != reach:
                    near_copy(way, layer, k).wait_send()

            def sent(step, carry, way=way, layer=layer):
                far_copy(way, layer, step).wait_send()
                return carry

            lax.fori_loop(1, peers, sent, 0)


def on_device(
    nodes,
    edges,
    near_table,
    far_table,
    edge_sender,
    edge_receiver,
    edge_w1,
    edge_b1,
    edge_w2,
    edge_gain,
    edge_shift,
    node_w1,
    node_b1,
    node_w2,
    node_gain,
    node_shift,
):
    peers = lax.axis_size(("node", "feat"))
    feat_size = lax.axis_size("feat")
    span, near_width = near_table.shape[1:]
    cap = far_table.shape[2]
    near_total = span * near_width
    near_table = jnp.transpose(near_table, (1, 0, 2))
    far_table = far_table.reshape(peers, cap).T
    slots = near_total + peers * cap
    padded = round_up(slots + 1, LANES)
    node_rows, features = nodes.shape
    edge_count = edges.shape[0]
    layers = edge_w1.shape[0]
    blocks = edge_count // BLOCK
    senders = edge_sender.reshape(edge_count // LANES, LANES)
    receivers = edge_receiver.reshape(edge_count // LANES, LANES)
    tile = cap * features // LANES
    bf16, f32 = jnp.bfloat16, jnp.float32
    sizes = (peers, feat_size, layers, span, near_width, cap, slots)
    vmem = pl.BlockSpec(memory_space=pltpu.VMEM)
    hbm = pl.BlockSpec(memory_space=pltpu.HBM)
    near_buffer = pltpu.VMEM((layers, padded, features), bf16)
    far_buffer = pltpu.VMEM((layers, peers, tile, LANES), f32)
    flops = 2 * layers * edge_count * features * (2 * features + 2 * padded + slots)
    return pl.pallas_call(
        functools.partial(kernel, sizes),
        out_shape=(
            jax.ShapeDtypeStruct(nodes.shape, bf16),
            jax.ShapeDtypeStruct(edges.shape, bf16),
        ),
        in_specs=[hbm] * 16,
        out_specs=(vmem, hbm),
        scratch_shapes=[
            pltpu.VMEM(edges.shape, bf16),
            pltpu.VMEM(near_table.shape, jnp.int32),
            pltpu.VMEM(far_table.shape, jnp.int32),
            pltpu.VMEM(senders.shape, jnp.int32),
            pltpu.VMEM(receivers.shape, jnp.int32),
        ]
        + [pltpu.VMEM(edge_b1.shape, f32)] * 6
        + [
            pltpu.VMEM(edge_w1.shape, bf16),
            pltpu.VMEM(edge_w2.shape, bf16),
            pltpu.VMEM(node_w1.shape, bf16),
            pltpu.VMEM(node_w2.shape, bf16),
            pltpu.VMEM(edges.shape, f32),
            pltpu.VMEM((BLOCK, features), bf16),
            pltpu.VMEM((BLOCK, features), bf16),
            pltpu.VMEM((edge_count, 2 * padded), bf16),
            pltpu.VMEM((blocks, round_up(slots, 16), BLOCK), bf16),
            pltpu.VMEM((padded, node_rows), f32),
            pltpu.VMEM((2 * padded, features), bf16),
            pltpu.VMEM((round_up(slots, 16), features), f32),
            near_buffer, near_buffer, near_buffer, near_buffer,
            far_buffer, far_buffer, far_buffer, far_buffer,
            pltpu.SemaphoreType.DMA((15 + layers,)),
            pltpu.SemaphoreType.DMA((blocks,)),
            pltpu.SemaphoreType.DMA((2 * layers * span,)),
            pltpu.SemaphoreType.DMA((2 * layers * span,)),
            pltpu.SemaphoreType.DMA((2 * layers * peers,)),
            pltpu.SemaphoreType.DMA((2 * layers * peers,)),
        ],
        compiler_params=pltpu.CompilerParams(
            collective_id=0, has_side_effects=True, vmem_limit_bytes=62 * 2**20
        ),
        cost_estimate=pl.CostEstimate(flops=flops, bytes_accessed=12 * 2**20, transcendentals=0),
    )(
        nodes, near_table, far_table, senders, receivers,
        edge_b1, edge_gain, edge_shift, node_b1, node_gain, node_shift,
        edges, edge_w1, edge_w2, node_w1, node_w2,
    )


def solution(mesh):
    split = P(AXES, None)
    table = P(AXES, None, None)
    return jax.shard_map(
        on_device,
        mesh=mesh,
        in_specs=(split, split, table, table, P(AXES), P(AXES)) + (P(),) * 10,
        out_specs=(split, split),
        check_vma=False,
    )
```

```python
import functools

import jax
import jax.numpy as jnp
from jax import lax
from jax.experimental import pallas as pl
from jax.experimental.pallas import tpu as pltpu
from jax.sharding import PartitionSpec as P

EPSILON = 1e-05
LANES = 128
BLOCK = 256
AXES = ("ens", "node", "feat")
MESH = pl.DeviceIdType.MESH


def round_up(value, multiple):
    return -(-value // multiple) * multiple


def dot(a, b):
    return jnp.dot(a, b, preferred_element_type=jnp.float32)


def layer_norm(center, norm_gain, norm_shift):
    spread = jnp.mean(center * center, axis=-1, keepdims=True)
    return center * lax.rsqrt(spread + EPSILON) * norm_gain + norm_shift


def gated(half):
    return (half + half * jnp.tanh(half)).astype(jnp.bfloat16)


def kernel(
    sizes,
    nodes_hbm, near_hbm, far_hbm, senders_hbm, receivers_hbm,
    edge_b1_hbm, edge_gain_hbm, edge_shift_hbm, node_b1_hbm, node_gain_hbm, node_shift_hbm,
    edges_hbm, edge_w1_hbm, edge_w2_hbm, node_w1_hbm, node_w2_hbm,
    states, edge_out,
    edges,
    near_table, far_table, senders, receivers,
    edge_b1, edge_gain, edge_shift, node_b1, node_gain, node_shift,
    edge_w1, edge_w2, node_w1, node_w2,
    partial, hidden_even, hidden_odd, hot, hot_t, pick, projected, sums,
    near_out, near_in, near_back_out, near_back_in,
    far_out, far_in, far_back_out, far_back_in,
    far_rows,
    load_sems, store_sems,
    near_send, near_recv, far_send, far_recv,
):
    peers, feat_size, layers, span, near_width, cap, slots = sizes
    reach = (span - 1) // 2
    near_total = span * near_width
    padded = pick.shape[0]
    features = states.shape[1]
    columns = features // LANES
    edge_count = edges.shape[0]
    blocks = edge_count // BLOCK
    ens = lax.axis_index("ens")
    me = lax.axis_index("node") * feat_size + lax.axis_index("feat")

    def device(index):
        return (ens, lax.div(index, feat_size), lax.rem(index, feat_size))

    def around(index):
        return jnp.where(index >= peers, index - peers, index)

    loads = []

    def load(source, target):
        copy = pltpu.make_async_copy(source, target, load_sems.at[len(loads)])
        copy.start()
        loads.append(copy)
        return copy

    first_loads = [load(nodes_hbm, states), load(near_hbm, near_table), load(far_hbm, far_table)]
    index_loads = [load(senders_hbm, senders), load(receivers_hbm, receivers)]
    own_loads = [load(edge_b1_hbm, edge_b1), load(edges_hbm, edges), load(edge_w1_hbm.at[0], edge_w1.at[0])]
    late_loads = [
        load(edge_gain_hbm, edge_gain),
        load(edge_shift_hbm, edge_shift),
        load(node_b1_hbm, node_b1),
        load(node_gain_hbm, node_gain),
        load(node_shift_hbm, node_shift),
        load(edge_w2_hbm, edge_w2),
        load(node_w1_hbm, node_w1),
        load(node_w2_hbm, node_w2),
    ]
    late_loads += [load(edge_w1_hbm.at[layer], edge_w1.at[layer]) for layer in range(1, layers)]

    barrier = pltpu.get_barrier_semaphore()

    def greet(step, carry):
        pl.semaphore_signal(barrier, inc=1, device_id=device(around(me + step)), device_id_type=MESH)
        return carry

    lax.fori_loop(1, peers, greet, 0)

    for copy in first_loads:
        copy.wait()
    node_rows = states.shape[0]
    near_ids = lax.broadcasted_iota(jnp.int32, (near_width, node_rows), 1).astype(jnp.float32)
    far_ids = lax.broadcasted_iota(jnp.int32, (peers, node_rows), 1).astype(jnp.float32)
    for k in range(span):
        row = near_table[k].astype(jnp.float32)
        column = jnp.transpose(jnp.broadcast_to(row, (node_rows, near_width)))
        pick[k * near_width : (k + 1) * near_width, :] = jnp.where(column == near_ids, 1.0, 0.0)
    for s in range(cap):
        begin = near_total + s * peers
        row = far_table[s : s + 1, :].astype(jnp.float32)
        column = jnp.transpose(jnp.broadcast_to(row, (node_rows, peers)))
        pick[begin : begin + peers, :] = jnp.where(column == far_ids, 1.0, 0.0)
    pick[slots:, :] = jnp.zeros((padded - slots, node_rows), jnp.float32)

    def near_copy(way, layer, k):
        source, target = ((near_out, near_in), (near_back_out, near_back_in))[way]
        rows = pl.ds(k * near_width, near_width)
        shift = (k - reach) if way == 0 else (reach - k)
        slot = (way * layers + layer) * span + k
        return pltpu.make_async_remote_copy(
            src_ref=source.at[layer, rows],
            dst_ref=target.at[layer, rows],
            send_sem=near_send.at[slot],
            recv_sem=near_recv.at[slot],
            device_id=device(around(me + (shift + peers) % peers)),
            device_id_type=MESH,
        )

    def far_copy(way, layer, step):
        source, target = ((far_out, far_in), (far_back_out, far_back_in))[way]
        to = around(me + step)
        slot = (way * layers + layer) * peers + step
        return pltpu.make_async_remote_copy(
            src_ref=source.at[layer, to],
            dst_ref=target.at[layer, me],
            send_sem=far_send.at[slot],
            recv_sem=far_recv.at[slot],
            device_id=device(to),
            device_id_type=MESH,
        )

    def far_arrival(way, layer, step):
        source, target = ((far_out, far_in), (far_back_out, far_back_in))[way]
        origin = around(me + peers - step)
        slot = (way * layers + layer) * peers + step
        return pltpu.make_async_remote_copy(
            src_ref=source.at[layer, origin],
            dst_ref=target.at[layer, origin],
            send_sem=far_send.at[slot],
            recv_sem=far_recv.at[slot],
            device_id=device(origin),
            device_id_type=MESH,
        )

    def send(way, layer, rows, first=False):
        source, far_source = ((near_out, far_out), (near_back_out, far_back_out))[way]
        target, far_target = ((near_in, far_in), (near_back_in, far_back_in))[way]
        source[layer, :near_total, :] = rows[:near_total].astype(jnp.bfloat16)
        for s in range(cap):
            begin = near_total + s * peers
            for c in range(columns):
                far_rows[:, s * columns + c, :] = rows[begin : begin + peers, c * LANES : (c + 1) * LANES]
        far_source[layer] = far_rows[...].astype(jnp.bfloat16)
        if first:
            pl.semaphore_wait(barrier, peers - 1)
        for k in range(span):
            if k != reach:
                near_copy(way, layer, k).start()

        def start(step, carry):
            far_copy(way, layer, step).start()
            return carry

        lax.fori_loop(1, peers, start, 0)
        own = slice(reach * near_width, (reach + 1) * near_width)
        target[layer, own, :] = source[layer, own, :]
        far_target[layer, pl.ds(me, 1)] = far_source[layer, pl.ds(me, 1)]
        target[layer, slots:, :] = jnp.zeros((padded - slots, features), jnp.bfloat16)

    def receive(way, layer):
        target, far_target = ((near_in, far_in), (near_back_in, far_back_in))[way]
        for k in range(span):
            if k != reach:
                near_copy(way, layer, k).wait_recv()

        def wait(step, carry):
            far_arrival(way, layer, step).wait_recv()
            return carry

        lax.fori_loop(1, peers, wait, 0)
        far_rows[...] = far_target[layer].astype(jnp.float32)
        for s in range(cap):
            begin = near_total + s * peers
            for c in range(columns):
                target[layer, begin : begin + peers, c * LANES : (c + 1) * LANES] = far_rows[
                    :, s * columns + c, :
                ].astype(jnp.bfloat16)

    def gathered():
        return dot(pick[...].astype(jnp.bfloat16), states[...])

    def store(i):
        rows = pl.ds(pl.multiple_of(i * BLOCK, BLOCK), BLOCK)
        return pltpu.make_async_copy(edges.at[rows], edge_out.at[rows], store_sems.at[i])

    send(0, 0, gathered(), first=True)

    def renumbered(index):
        value = index.astype(jnp.float32)
        far = value - near_total
        peer = jnp.floor((far + 0.5) * (1.0 / cap))
        return jnp.where(value < near_total, value, near_total + (far - peer * cap) * peers + peer)

    for copy in index_loads:
        copy.wait()
    sender_ids = renumbered(senders[...])
    receiver_ids = renumbered(receivers[...])
    lane_ids = lax.broadcasted_iota(jnp.int32, (LANES, LANES), 1).astype(jnp.float32)
    slot_ids = lax.broadcasted_iota(jnp.int32, (hot_t.shape[1], LANES), 0).astype(jnp.float32)
    for b in range(edge_count // LANES):
        rows = slice(b * LANES, (b + 1) * LANES)
        for side, ids in enumerate((sender_ids, receiver_ids)):
            column = jnp.transpose(jnp.broadcast_to(ids[b : b + 1], (LANES, LANES)))
            for j in range(padded // LANES):
                begin = side * padded + j * LANES
                hot[rows, begin : begin + LANES] = jnp.where(column == lane_ids + j * LANES, 1.0, 0.0).astype(
                    jnp.bfloat16
                )
        begin = (b * LANES) % BLOCK
        hot_t[b * LANES // BLOCK, :, begin : begin + LANES] = jnp.where(
            receiver_ids[b : b + 1] == slot_ids, 1.0, 0.0
        ).astype(jnp.bfloat16)

    for copy in own_loads:
        copy.wait()
    for layer in range(layers):

        def own_term(i, carry, layer=layer):
            rows = pl.ds(pl.multiple_of(i * BLOCK, BLOCK), BLOCK)
            partial[rows, :] = 0.5 * (
                dot(edges[rows, :], edge_w1[layer, :features, :]) + edge_b1[layer : layer + 1, :]
            )
            return carry

        if layer == 0:
            lax.fori_loop(0, blocks, own_term, 0)
            for copy in late_loads:
                copy.wait()
            for weight in (edge_w2, node_w2):
                for place in range(layers):
                    values = weight[place].astype(jnp.float32)
                    weight[place] = (values - jnp.mean(values, axis=-1, keepdims=True)).astype(jnp.bfloat16)

        receive(0, layer)
        arrived = near_in[layer]
        for side in range(2):
            begin = (1 + side) * features
            projected[side * padded : (side + 1) * padded, :] = (
                0.5 * dot(arrived, edge_w1[layer, begin : begin + features, :])
            ).astype(jnp.bfloat16)

        sums[...] = jnp.zeros_like(sums)

        def block_rows(i):
            return pl.ds(pl.multiple_of(i * BLOCK, BLOCK), BLOCK)

        def first_half(i, hidden):
            rows = block_rows(i)
            hidden[...] = gated(partial[rows, :] + dot(hot[rows, :], projected[...]))

        def second_half(i, hidden, layer=layer):
            rows = block_rows(i)
            mixed = dot(hidden[...], edge_w2[layer])
            fresh = edges[rows, :].astype(jnp.float32) + layer_norm(
                mixed, edge_gain[layer : layer + 1, :], edge_shift[layer : layer + 1, :]
            )
            fresh = fresh.astype(jnp.bfloat16)
            edges[rows, :] = fresh
            if layer == layers - 1:
                store(i).start()
            sums[...] += dot(hot_t[i], fresh)

        first_half(0, hidden_even)

        def update(j, carry):
            first_half(2 * j + 1, hidden_odd)
            second_half(2 * j, hidden_even)
            first_half(2 * j + 2, hidden_even)
            second_half(2 * j + 1, hidden_odd)
            return carry

        lax.fori_loop(0, blocks // 2 - 1, update, 0)
        first_half(blocks - 1, hidden_odd)
        second_half(blocks - 2, hidden_even)
        second_half(blocks - 1, hidden_odd)

        send(1, layer, sums)
        pre = dot(states[...], node_w1[layer, :features, :]) + node_b1[layer : layer + 1, :]
        if layer + 1 < layers:
            lax.fori_loop(0, blocks, functools.partial(own_term, layer=layer + 1), 0)
        receive(1, layer)
        aggregate = dot(jnp.transpose(pick[...]).astype(jnp.bfloat16), near_back_in[layer]).astype(jnp.bfloat16)
        half = 0.5 * (pre + dot(aggregate, node_w1[layer, features:, :]))
        mixed = dot(gated(half), node_w2[layer])
        fresh = states[...].astype(jnp.float32) + layer_norm(
            mixed, node_gain[layer : layer + 1, :], node_shift[layer : layer + 1, :]
        )
        states[...] = fresh.astype(jnp.bfloat16)
        if layer + 1 < layers:
            send(0, layer + 1, gathered())

    def drain(i, carry):
        store(i).wait()
        return carry

    lax.fori_loop(0, blocks, drain, 0)
    for way in range(2):
        for layer in range(layers):
            for k in range(span):
                if k != reach:
                    near_copy(way, layer, k).wait_send()

            def sent(step, carry, way=way, layer=layer):
                far_copy(way, layer, step).wait_send()
                return carry

            lax.fori_loop(1, peers, sent, 0)


def handed_on(nodes_in, edges_in, nodes_out, edges_out, nodes_held, edges_held, sems):
    pieces = [(nodes_in, nodes_held, nodes_out)]
    for begin in range(0, edges_in.shape[0], BLOCK):
        rows = pl.ds(begin, BLOCK)
        pieces.append((edges_in.at[rows], edges_held.at[rows], edges_out.at[rows]))
    fetches = [pltpu.make_async_copy(a, b, sems.at[0, i]) for i, (a, b, _) in enumerate(pieces)]
    writes = [pltpu.make_async_copy(b, c, sems.at[1, i]) for i, (_, b, c) in enumerate(pieces)]
    for fetch in fetches:
        fetch.start()
    for fetch, write in zip(fetches, writes):
        fetch.wait()
        write.start()
    for write in writes:
        write.wait()


def on_device(
    nodes,
    edges,
    near_table,
    far_table,
    edge_sender,
    edge_receiver,
    edge_w1,
    edge_b1,
    edge_w2,
    edge_gain,
    edge_shift,
    node_w1,
    node_b1,
    node_w2,
    node_gain,
    node_shift,
):
    peers = lax.axis_size(("node", "feat"))
    feat_size = lax.axis_size("feat")
    span, near_width = near_table.shape[1:]
    cap = far_table.shape[2]
    near_total = span * near_width
    near_table = jnp.transpose(near_table, (1, 0, 2))
    far_table = far_table.reshape(peers, cap).T
    slots = near_total + peers * cap
    padded = round_up(slots + 1, LANES)
    node_rows, features = nodes.shape
    edge_count = edges.shape[0]
    layers = edge_w1.shape[0]
    blocks = edge_count // BLOCK
    senders = edge_sender.reshape(edge_count // LANES, LANES)
    receivers = edge_receiver.reshape(edge_count // LANES, LANES)
    tile = cap * features // LANES
    bf16, f32 = jnp.bfloat16, jnp.float32
    sizes = (peers, feat_size, layers, span, near_width, cap, slots)
    vmem = pl.BlockSpec(memory_space=pltpu.VMEM)
    hbm = pl.BlockSpec(memory_space=pltpu.HBM)
    near_buffer = pltpu.VMEM((layers, padded, features), bf16)
    far_buffer = pltpu.VMEM((layers, peers, tile, LANES), bf16)
    flops = 2 * layers * edge_count * features * (2 * features + 2 * padded + slots)
    out_shape = (
        jax.ShapeDtypeStruct(nodes.shape, bf16),
        jax.ShapeDtypeStruct(edges.shape, bf16),
    )
    results = pl.pallas_call(
        functools.partial(kernel, sizes),
        out_shape=out_shape,
        in_specs=[hbm] * 16,
        out_specs=(vmem, hbm),
        scratch_shapes=[
            pltpu.VMEM(edges.shape, bf16),
            pltpu.VMEM(near_table.shape, jnp.int32),
            pltpu.VMEM(far_table.shape, jnp.int32),
            pltpu.VMEM(senders.shape, jnp.int32),
            pltpu.VMEM(receivers.shape, jnp.int32),
        ]
        + [pltpu.VMEM(edge_b1.shape, f32)] * 6
        + [
            pltpu.VMEM(edge_w1.shape, bf16),
            pltpu.VMEM(edge_w2.shape, bf16),
            pltpu.VMEM(node_w1.shape, bf16),
            pltpu.VMEM(node_w2.shape, bf16),
            pltpu.VMEM(edges.shape, f32),
            pltpu.VMEM((BLOCK, features), bf16),
            pltpu.VMEM((BLOCK, features), bf16),
            pltpu.VMEM((edge_count, 2 * padded), bf16),
            pltpu.VMEM((blocks, round_up(slots, 16), BLOCK), bf16),
            pltpu.VMEM((padded, node_rows), f32),
            pltpu.VMEM((2 * padded, features), bf16),
            pltpu.VMEM((round_up(slots, 16), features), f32),
            near_buffer, near_buffer, near_buffer, near_buffer,
            far_buffer, far_buffer, far_buffer, far_buffer,
            pltpu.VMEM((peers, tile, LANES), f32),
            pltpu.SemaphoreType.DMA((15 + layers,)),
            pltpu.SemaphoreType.DMA((blocks,)),
            pltpu.SemaphoreType.DMA((2 * layers * span,)),
            pltpu.SemaphoreType.DMA((2 * layers * span,)),
            pltpu.SemaphoreType.DMA((2 * layers * peers,)),
            pltpu.SemaphoreType.DMA((2 * layers * peers,)),
        ],
        compiler_params=pltpu.CompilerParams(
            collective_id=0, has_side_effects=True, vmem_limit_bytes=62 * 2**20
        ),
        cost_estimate=pl.CostEstimate(flops=flops, bytes_accessed=12 * 2**20, transcendentals=0),
    )(
        nodes, near_table, far_table, senders, receivers,
        edge_b1, edge_gain, edge_shift, node_b1, node_gain, node_shift,
        edges, edge_w1, edge_w2, node_w1, node_w2,
    )
    return pl.pallas_call(
        handed_on,
        out_shape=out_shape,
        in_specs=[hbm] * 2,
        out_specs=(hbm, hbm),
        scratch_shapes=[
            pltpu.VMEM(nodes.shape, bf16),
            pltpu.VMEM(edges.shape, bf16),
            pltpu.SemaphoreType.DMA((2, 1 + blocks)),
        ],
        compiler_params=pltpu.CompilerParams(vmem_limit_bytes=62 * 2**20),
        cost_estimate=pl.CostEstimate(flops=0, bytes_accessed=2 * 2 * (nodes.size + edges.size), transcendentals=0),
    )(*results)


def solution(mesh):
    split = P(AXES, None)
    table = P(AXES, None, None)
    return jax.shard_map(
        on_device,
        mesh=mesh,
        in_specs=(split, split, table, table, P(AXES), P(AXES)) + (P(),) * 10,
        out_specs=(split, split),
        check_vma=False,
    )
```

```python
import functools

import jax
import jax.numpy as jnp
from jax import lax
from jax.experimental import pallas as pl
from jax.experimental.pallas import tpu as pltpu
from jax.sharding import PartitionSpec as P

EPSILON = 1e-05
LANES = 128
BLOCK = 512
AXES = ("ens", "node", "feat")
MESH = pl.DeviceIdType.MESH


def round_up(value, multiple):
    return -(-value // multiple) * multiple


def dot(a, b):
    return jnp.dot(a, b, preferred_element_type=jnp.float32)


def layer_norm(center, norm_gain, norm_shift):
    spread = jnp.mean(center * center, axis=-1, keepdims=True)
    return center * lax.rsqrt(spread + EPSILON) * norm_gain + norm_shift


def gated(half):
    return (half + half * jnp.tanh(half)).astype(jnp.bfloat16)


def kernel(
    sizes,
    nodes_hbm, near_hbm, far_hbm, senders_hbm, receivers_hbm,
    edge_b1_hbm, edge_gain_hbm, edge_shift_hbm, node_b1_hbm, node_gain_hbm, node_shift_hbm,
    edges_hbm, edge_w1_hbm, edge_w2_hbm, node_w1_hbm, node_w2_hbm,
    states, edge_out,
    edges,
    near_table, far_table, senders, receivers,
    edge_b1, edge_gain, edge_shift, node_b1, node_gain, node_shift,
    edge_w1, edge_w2, node_w1, node_w2,
    partial, hidden_even, hidden_odd, hot, hot_t, pick, projected, sums,
    near_out, near_in, near_back_out, near_back_in,
    far_out, far_in, far_back_out, far_back_in,
    far_rows,
    load_sems, store_sems,
    near_send, near_recv, far_send, far_recv,
):
    peers, feat_size, layers, span, near_width, cap, slots = sizes
    reach = (span - 1) // 2
    near_total = span * near_width
    padded = pick.shape[0]
    features = states.shape[1]
    columns = features // LANES
    edge_count = edges.shape[0]
    blocks = edge_count // BLOCK
    ens = lax.axis_index("ens")
    me = lax.axis_index("node") * feat_size + lax.axis_index("feat")

    def device(index):
        return (ens, lax.div(index, feat_size), lax.rem(index, feat_size))

    def around(index):
        return jnp.where(index >= peers, index - peers, index)

    loads = []

    def load(source, target):
        copy = pltpu.make_async_copy(source, target, load_sems.at[len(loads)])
        copy.start()
        loads.append(copy)
        return copy

    first_loads = [load(nodes_hbm, states), load(near_hbm, near_table), load(far_hbm, far_table)]
    index_loads = [load(senders_hbm, senders), load(receivers_hbm, receivers)]
    own_loads = [load(edge_b1_hbm, edge_b1), load(edges_hbm, edges), load(edge_w1_hbm.at[0], edge_w1.at[0])]
    late_loads = [
        load(edge_gain_hbm, edge_gain),
        load(edge_shift_hbm, edge_shift),
        load(node_b1_hbm, node_b1),
        load(node_gain_hbm, node_gain),
        load(node_shift_hbm, node_shift),
        load(edge_w2_hbm, edge_w2),
        load(node_w1_hbm, node_w1),
        load(node_w2_hbm, node_w2),
    ]
    late_loads += [load(edge_w1_hbm.at[layer], edge_w1.at[layer]) for layer in range(1, layers)]

    barrier = pltpu.get_barrier_semaphore()

    def greet(step, carry):
        pl.semaphore_signal(barrier, inc=1, device_id=device(around(me + step)), device_id_type=MESH)
        return carry

    lax.fori_loop(1, peers, greet, 0)

    for copy in first_loads:
        copy.wait()
    node_rows = states.shape[0]
    near_ids = lax.broadcasted_iota(jnp.int32, (near_width, node_rows), 1).astype(jnp.float32)
    far_ids = lax.broadcasted_iota(jnp.int32, (peers, node_rows), 1).astype(jnp.float32)
    for k in range(span):
        row = near_table[k].astype(jnp.float32)
        column = jnp.transpose(jnp.broadcast_to(row, (node_rows, near_width)))
        pick[k * near_width : (k + 1) * near_width, :] = jnp.where(column == near_ids, 1.0, 0.0)
    for s in range(cap):
        begin = near_total + s * peers
        row = far_table[s : s + 1, :].astype(jnp.float32)
        column = jnp.transpose(jnp.broadcast_to(row, (node_rows, peers)))
        pick[begin : begin + peers, :] = jnp.where(column == far_ids, 1.0, 0.0)
    pick[slots:, :] = jnp.zeros((padded - slots, node_rows), jnp.float32)

    def near_copy(way, layer, k):
        source, target = ((near_out, near_in), (near_back_out, near_back_in))[way]
        rows = pl.ds(k * near_width, near_width)
        shift = (k - reach) if way == 0 else (reach - k)
        slot = (way * layers + layer) * span + k
        return pltpu.make_async_remote_copy(
            src_ref=source.at[layer, rows],
            dst_ref=target.at[layer, rows],
            send_sem=near_send.at[slot],
            recv_sem=near_recv.at[slot],
            device_id=device(around(me + (shift + peers) % peers)),
            device_id_type=MESH,
        )

    def far_copy(way, layer, step):
        source, target = ((far_out, far_in), (far_back_out, far_back_in))[way]
        to = around(me + step)
        slot = (way * layers + layer) * peers + step
        return pltpu.make_async_remote_copy(
            src_ref=source.at[layer, to],
            dst_ref=target.at[layer, me],
            send_sem=far_send.at[slot],
            recv_sem=far_recv.at[slot],
            device_id=device(to),
            device_id_type=MESH,
        )

    def far_arrival(way, layer, step):
        source, target = ((far_out, far_in), (far_back_out, far_back_in))[way]
        origin = around(me + peers - step)
        slot = (way * layers + layer) * peers + step
        return pltpu.make_async_remote_copy(
            src_ref=source.at[layer, origin],
            dst_ref=target.at[layer, origin],
            send_sem=far_send.at[slot],
            recv_sem=far_recv.at[slot],
            device_id=device(origin),
            device_id_type=MESH,
        )

    def send(way, layer, rows, first=False):
        source, far_source = ((near_out, far_out), (near_back_out, far_back_out))[way]
        target, far_target = ((near_in, far_in), (near_back_in, far_back_in))[way]
        source[layer, :near_total, :] = rows[:near_total].astype(jnp.bfloat16)
        for s in range(cap):
            begin = near_total + s * peers
            for c in range(columns):
                far_rows[:, s * columns + c, :] = rows[begin : begin + peers, c * LANES : (c + 1) * LANES]
        far_source[layer] = far_rows[...].astype(jnp.bfloat16)
        if first:
            pl.semaphore_wait(barrier, peers - 1)
        for k in range(span):
            if k != reach:
                near_copy(way, layer, k).start()

        def start(step, carry):
            far_copy(way, layer, step).start()
            return carry

        lax.fori_loop(1, peers, start, 0)
        own = slice(reach * near_width, (reach + 1) * near_width)
        target[layer, own, :] = source[layer, own, :]
        far_target[layer, pl.ds(me, 1)] = far_source[layer, pl.ds(me, 1)]
        target[layer, slots:, :] = jnp.zeros((padded - slots, features), jnp.bfloat16)

    def receive(way, layer):
        target, far_target = ((near_in, far_in), (near_back_in, far_back_in))[way]
        for k in range(span):
            if k != reach:
                near_copy(way, layer, k).wait_recv()

        def wait(step, carry):
            far_arrival(way, layer, step).wait_recv()
            return carry

        lax.fori_loop(1, peers, wait, 0)
        far_rows[...] = far_target[layer].astype(jnp.float32)
        for s in range(cap):
            begin = near_total + s * peers
            for c in range(columns):
                target[layer, begin : begin + peers, c * LANES : (c + 1) * LANES] = far_rows[
                    :, s * columns + c, :
                ].astype(jnp.bfloat16)

    def gathered():
        return dot(pick[...].astype(jnp.bfloat16), states[...])

    def store(i):
        rows = pl.ds(i * BLOCK, BLOCK)
        return pltpu.make_async_copy(edges.at[rows], edge_out.at[rows], store_sems.at[i])

    send(0, 0, gathered(), first=True)

    def renumbered(index):
        value = index.astype(jnp.float32)
        far = value - near_total
        peer = jnp.floor((far + 0.5) * (1.0 / cap))
        return jnp.where(value < near_total, value, near_total + (far - peer * cap) * peers + peer)

    for copy in index_loads:
        copy.wait()
    sender_ids = renumbered(senders[...])
    receiver_ids = renumbered(receivers[...])
    lane_ids = lax.broadcasted_iota(jnp.int32, (LANES, LANES), 1).astype(jnp.float32)
    slot_ids = lax.broadcasted_iota(jnp.int32, (hot_t.shape[1], LANES), 0).astype(jnp.float32)
    for b in range(edge_count // LANES):
        rows = slice(b * LANES, (b + 1) * LANES)
        for side, ids in enumerate((sender_ids, receiver_ids)):
            column = jnp.transpose(jnp.broadcast_to(ids[b : b + 1], (LANES, LANES)))
            for j in range(padded // LANES):
                begin = side * padded + j * LANES
                hot[rows, begin : begin + LANES] = jnp.where(column == lane_ids + j * LANES, 1.0, 0.0).astype(
                    jnp.bfloat16
                )
        begin = (b * LANES) % BLOCK
        hot_t[b * LANES // BLOCK, :, begin : begin + LANES] = jnp.where(
            receiver_ids[b : b + 1] == slot_ids, 1.0, 0.0
        ).astype(jnp.bfloat16)

    for copy in own_loads:
        copy.wait()
    for layer in range(layers):

        def own_term(i, carry, layer=layer):
            rows = pl.ds(pl.multiple_of(i * BLOCK, BLOCK), BLOCK)
            partial[rows, :] = 0.5 * (
                dot(edges[rows, :], edge_w1[layer, :features, :]) + edge_b1[layer : layer + 1, :]
            )
            return carry

        if layer == 0:
            lax.fori_loop(0, blocks, own_term, 0)
            for copy in late_loads:
                copy.wait()
            for weight in (edge_w2, node_w2):
                for place in range(layers):
                    values = weight[place].astype(jnp.float32)
                    weight[place] = (values - jnp.mean(values, axis=-1, keepdims=True)).astype(jnp.bfloat16)

        receive(0, layer)
        arrived = near_in[layer]
        for side in range(2):
            begin = (1 + side) * features
            projected[side * padded : (side + 1) * padded, :] = (
                0.5 * dot(arrived, edge_w1[layer, begin : begin + features, :])
            ).astype(jnp.bfloat16)

        sums[...] = jnp.zeros_like(sums)

        def block_rows(i):
            return pl.ds(i * BLOCK, BLOCK)

        def first_half(i, hidden):
            rows = block_rows(i)
            hidden[...] = gated(partial[rows, :] + dot(hot[rows, :], projected[...]))

        def second_half(i, hidden, layer=layer):
            rows = block_rows(i)
            mixed = dot(hidden[...], edge_w2[layer])
            fresh = edges[rows, :].astype(jnp.float32) + layer_norm(
                mixed, edge_gain[layer : layer + 1, :], edge_shift[layer : layer + 1, :]
            )
            fresh = fresh.astype(jnp.bfloat16)
            edges[rows, :] = fresh
            if layer == layers - 1:
                store(i).start()
            sums[...] += dot(hot_t[i], fresh)

        held = (hidden_even, hidden_odd)
        first_half(0, held[0])
        for i in range(blocks):
            if i + 1 < blocks:
                first_half(i + 1, held[(i + 1) % 2])
            second_half(i, held[i % 2])

        send(1, layer, sums)
        pre = dot(states[...], node_w1[layer, :features, :]) + node_b1[layer : layer + 1, :]
        if layer + 1 < layers:
            lax.fori_loop(0, blocks, functools.partial(own_term, layer=layer + 1), 0)
        receive(1, layer)
        aggregate = dot(jnp.transpose(pick[...]).astype(jnp.bfloat16), near_back_in[layer]).astype(jnp.bfloat16)
        half = 0.5 * (pre + dot(aggregate, node_w1[layer, features:, :]))
        mixed = dot(gated(half), node_w2[layer])
        fresh = states[...].astype(jnp.float32) + layer_norm(
            mixed, node_gain[layer : layer + 1, :], node_shift[layer : layer + 1, :]
        )
        states[...] = fresh.astype(jnp.bfloat16)
        if layer + 1 < layers:
            send(0, layer + 1, gathered())

    for i in range(blocks):
        store(i).wait()
    for way in range(2):
        for layer in range(layers):
            for k in range(span):
                if k != reach:
                    near_copy(way, layer, k).wait_send()

            def sent(step, carry, way=way, layer=layer):
                far_copy(way, layer, step).wait_send()
                return carry

            lax.fori_loop(1, peers, sent, 0)


def handed_on(nodes_in, edges_in, nodes_out, edges_out, nodes_held, edges_held, sems):
    pieces = [(nodes_in, nodes_held, nodes_out)]
    for begin in range(0, edges_in.shape[0], BLOCK):
        rows = pl.ds(begin, BLOCK)
        pieces.append((edges_in.at[rows], edges_held.at[rows], edges_out.at[rows]))
    fetches = [pltpu.make_async_copy(a, b, sems.at[0, i]) for i, (a, b, _) in enumerate(pieces)]
    writes = [pltpu.make_async_copy(b, c, sems.at[1, i]) for i, (_, b, c) in enumerate(pieces)]
    for fetch in fetches:
        fetch.start()
    for fetch, write in zip(fetches, writes):
        fetch.wait()
        write.start()
    for write in writes:
        write.wait()


def on_device(
    nodes,
    edges,
    near_table,
    far_table,
    edge_sender,
    edge_receiver,
    edge_w1,
    edge_b1,
    edge_w2,
    edge_gain,
    edge_shift,
    node_w1,
    node_b1,
    node_w2,
    node_gain,
    node_shift,
):
    peers = lax.axis_size(("node", "feat"))
    feat_size = lax.axis_size("feat")
    span, near_width = near_table.shape[1:]
    cap = far_table.shape[2]
    near_total = span * near_width
    near_table = jnp.transpose(near_table, (1, 0, 2))
    far_table = far_table.reshape(peers, cap).T
    slots = near_total + peers * cap
    padded = round_up(slots + 1, LANES)
    node_rows, features = nodes.shape
    edge_count = edges.shape[0]
    layers = edge_w1.shape[0]
    blocks = edge_count // BLOCK
    senders = edge_sender.reshape(edge_count // LANES, LANES)
    receivers = edge_receiver.reshape(edge_count // LANES, LANES)
    tile = cap * features // LANES
    bf16, f32 = jnp.bfloat16, jnp.float32
    sizes = (peers, feat_size, layers, span, near_width, cap, slots)
    vmem = pl.BlockSpec(memory_space=pltpu.VMEM)
    hbm = pl.BlockSpec(memory_space=pltpu.HBM)
    near_buffer = pltpu.VMEM((layers, padded, features), bf16)
    far_buffer = pltpu.VMEM((layers, peers, tile, LANES), bf16)
    flops = 2 * layers * edge_count * features * (2 * features + 2 * padded + slots)
    out_shape = (
        jax.ShapeDtypeStruct(nodes.shape, bf16),
        jax.ShapeDtypeStruct(edges.shape, bf16),
    )
    results = pl.pallas_call(
        functools.partial(kernel, sizes),
        out_shape=out_shape,
        in_specs=[hbm] * 16,
        out_specs=(vmem, hbm),
        scratch_shapes=[
            pltpu.VMEM(edges.shape, bf16),
            pltpu.VMEM(near_table.shape, jnp.int32),
            pltpu.VMEM(far_table.shape, jnp.int32),
            pltpu.VMEM(senders.shape, jnp.int32),
            pltpu.VMEM(receivers.shape, jnp.int32),
        ]
        + [pltpu.VMEM(edge_b1.shape, f32)] * 6
        + [
            pltpu.VMEM(edge_w1.shape, bf16),
            pltpu.VMEM(edge_w2.shape, bf16),
            pltpu.VMEM(node_w1.shape, bf16),
            pltpu.VMEM(node_w2.shape, bf16),
            pltpu.VMEM(edges.shape, f32),
            pltpu.VMEM((BLOCK, features), bf16),
            pltpu.VMEM((BLOCK, features), bf16),
            pltpu.VMEM((edge_count, 2 * padded), bf16),
            pltpu.VMEM((blocks, round_up(slots, 16), BLOCK), bf16),
            pltpu.VMEM((padded, node_rows), f32),
            pltpu.VMEM((2 * padded, features), bf16),
            pltpu.VMEM((round_up(slots, 16), features), f32),
            near_buffer, near_buffer, near_buffer, near_buffer,
            far_buffer, far_buffer, far_buffer, far_buffer,
            pltpu.VMEM((peers, tile, LANES), f32),
            pltpu.SemaphoreType.DMA((15 + layers,)),
            pltpu.SemaphoreType.DMA((blocks,)),
            pltpu.SemaphoreType.DMA((2 * layers * span,)),
            pltpu.SemaphoreType.DMA((2 * layers * span,)),
            pltpu.SemaphoreType.DMA((2 * layers * peers,)),
            pltpu.SemaphoreType.DMA((2 * layers * peers,)),
        ],
        compiler_params=pltpu.CompilerParams(
            collective_id=0, has_side_effects=True, vmem_limit_bytes=62 * 2**20
        ),
        cost_estimate=pl.CostEstimate(flops=flops, bytes_accessed=12 * 2**20, transcendentals=0),
    )(
        nodes, near_table, far_table, senders, receivers,
        edge_b1, edge_gain, edge_shift, node_b1, node_gain, node_shift,
        edges, edge_w1, edge_w2, node_w1, node_w2,
    )
    return pl.pallas_call(
        handed_on,
        out_shape=out_shape,
        in_specs=[hbm] * 2,
        out_specs=(hbm, hbm),
        scratch_shapes=[
            pltpu.VMEM(nodes.shape, bf16),
            pltpu.VMEM(edges.shape, bf16),
            pltpu.SemaphoreType.DMA((2, 1 + blocks)),
        ],
        compiler_params=pltpu.CompilerParams(vmem_limit_bytes=62 * 2**20),
        cost_estimate=pl.CostEstimate(flops=0, bytes_accessed=2 * 2 * (nodes.size + edges.size), transcendentals=0),
    )(*results)


def solution(mesh):
    split = P(AXES, None)
    table = P(AXES, None, None)
    return jax.shard_map(
        on_device,
        mesh=mesh,
        in_specs=(split, split, table, table, P(AXES), P(AXES)) + (P(),) * 10,
        out_specs=(split, split),
        check_vma=False,
    )
```

```python
import functools

import jax
import jax.numpy as jnp
from jax import lax
from jax.experimental import pallas as pl
from jax.experimental.pallas import tpu as pltpu
from jax.sharding import PartitionSpec as P

EPSILON = 1e-05
LANES = 128
BLOCK = 512
OWN_BLOCK = 1024
AXES = ("ens", "node", "feat")
MESH = pl.DeviceIdType.MESH


def round_up(value, multiple):
    return -(-value // multiple) * multiple


def dot(a, b):
    return jnp.dot(a, b, preferred_element_type=jnp.float32)


def layer_norm(center, norm_gain, norm_shift):
    spread = jnp.mean(center * center, axis=-1, keepdims=True)
    return center * lax.rsqrt(spread + EPSILON) * norm_gain + norm_shift


def gated(half):
    return (half + half * jnp.tanh(half)).astype(jnp.bfloat16)


def kernel(
    sizes,
    nodes_hbm, near_hbm, far_hbm, senders_hbm, receivers_hbm,
    edge_b1_hbm, edge_gain_hbm, edge_shift_hbm, node_b1_hbm, node_gain_hbm, node_shift_hbm,
    edges_hbm, edge_w1_hbm, edge_w2_hbm, node_w1_hbm, node_w2_hbm,
    states, edge_out,
    edges,
    near_table, far_table, senders, receivers,
    edge_b1, edge_gain, edge_shift, node_b1, node_gain, node_shift,
    edge_w1, edge_w2, node_w1, node_w2,
    partial, hidden_even, hidden_odd, hot, hot_t, pick, projected, sums,
    near_out, near_in, near_back_out, near_back_in,
    far_out, far_in, far_back_out, far_back_in,
    far_rows,
    load_sems, store_sems,
    near_send, near_recv, far_send, far_recv,
):
    peers, feat_size, layers, span, near_width, cap, slots = sizes
    reach = (span - 1) // 2
    near_total = span * near_width
    padded = pick.shape[0]
    features = states.shape[1]
    columns = features // LANES
    edge_count = edges.shape[0]
    blocks = edge_count // BLOCK
    own_blocks = edge_count // OWN_BLOCK
    ens = lax.axis_index("ens")
    me = lax.axis_index("node") * feat_size + lax.axis_index("feat")

    def device(index):
        return (ens, lax.div(index, feat_size), lax.rem(index, feat_size))

    def around(index):
        return jnp.where(index >= peers, index - peers, index)

    loads = []

    def load(source, target):
        copy = pltpu.make_async_copy(source, target, load_sems.at[len(loads)])
        copy.start()
        loads.append(copy)
        return copy

    first_loads = [load(nodes_hbm, states), load(near_hbm, near_table), load(far_hbm, far_table)]
    index_loads = [load(senders_hbm, senders), load(receivers_hbm, receivers)]
    own_loads = [load(edge_b1_hbm, edge_b1), load(edges_hbm, edges), load(edge_w1_hbm.at[0], edge_w1.at[0])]
    late_loads = [
        load(edge_gain_hbm, edge_gain),
        load(edge_shift_hbm, edge_shift),
        load(node_b1_hbm, node_b1),
        load(node_gain_hbm, node_gain),
        load(node_shift_hbm, node_shift),
        load(edge_w2_hbm, edge_w2),
        load(node_w1_hbm, node_w1),
        load(node_w2_hbm, node_w2),
    ]
    late_loads += [load(edge_w1_hbm.at[layer], edge_w1.at[layer]) for layer in range(1, layers)]

    barrier = pltpu.get_barrier_semaphore()

    def greet(step, carry):
        pl.semaphore_signal(barrier, inc=1, device_id=device(around(me + step)), device_id_type=MESH)
        return carry

    lax.fori_loop(1, peers, greet, 0)

    for copy in first_loads:
        copy.wait()
    node_rows = states.shape[0]
    near_ids = lax.broadcasted_iota(jnp.int32, (near_width, node_rows), 1).astype(jnp.float32)
    far_ids = lax.broadcasted_iota(jnp.int32, (peers, node_rows), 1).astype(jnp.float32)
    for k in range(span):
        row = near_table[k].astype(jnp.float32)
        column = jnp.transpose(jnp.broadcast_to(row, (node_rows, near_width)))
        pick[k * near_width : (k + 1) * near_width, :] = jnp.where(column == near_ids, 1.0, 0.0)
    for s in range(cap):
        begin = near_total + s * peers
        row = far_table[s : s + 1, :].astype(jnp.float32)
        column = jnp.transpose(jnp.broadcast_to(row, (node_rows, peers)))
        pick[begin : begin + peers, :] = jnp.where(column == far_ids, 1.0, 0.0)
    pick[slots:, :] = jnp.zeros((padded - slots, node_rows), jnp.float32)

    def near_copy(way, layer, k):
        source, target = ((near_out, near_in), (near_back_out, near_back_in))[way]
        rows = pl.ds(k * near_width, near_width)
        shift = (k - reach) if way == 0 else (reach - k)
        slot = (way * layers + layer) * span + k
        return pltpu.make_async_remote_copy(
            src_ref=source.at[layer, rows],
            dst_ref=target.at[layer, rows],
            send_sem=near_send.at[slot],
            recv_sem=near_recv.at[slot],
            device_id=device(around(me + (shift + peers) % peers)),
            device_id_type=MESH,
        )

    def far_copy(way, layer, step):
        source, target = ((far_out, far_in), (far_back_out, far_back_in))[way]
        to = around(me + step)
        slot = (way * layers + layer) * peers + step
        return pltpu.make_async_remote_copy(
            src_ref=source.at[layer, to],
            dst_ref=target.at[layer, me],
            send_sem=far_send.at[slot],
            recv_sem=far_recv.at[slot],
            device_id=device(to),
            device_id_type=MESH,
        )

    def far_arrival(way, layer, step):
        source, target = ((far_out, far_in), (far_back_out, far_back_in))[way]
        origin = around(me + peers - step)
        slot = (way * layers + layer) * peers + step
        return pltpu.make_async_remote_copy(
            src_ref=source.at[layer, origin],
            dst_ref=target.at[layer, origin],
            send_sem=far_send.at[slot],
            recv_sem=far_recv.at[slot],
            device_id=device(origin),
            device_id_type=MESH,
        )

    def send(way, layer, rows, first=False):
        source, far_source = ((near_out, far_out), (near_back_out, far_back_out))[way]
        target, far_target = ((near_in, far_in), (near_back_in, far_back_in))[way]
        source[layer, :near_total, :] = rows[:near_total].astype(jnp.bfloat16)
        if first:
            pl.semaphore_wait(barrier, peers - 1)
        for k in range(span):
            if k != reach:
                near_copy(way, layer, k).start()
        for s in range(cap):
            begin = near_total + s * peers
            for c in range(columns):
                far_rows[:, s * columns + c, :] = rows[begin : begin + peers, c * LANES : (c + 1) * LANES]
        far_source[layer] = far_rows[...].astype(jnp.bfloat16)

        def start(step, carry):
            far_copy(way, layer, step).start()
            return carry

        lax.fori_loop(1, peers, start, 0)
        own = slice(reach * near_width, (reach + 1) * near_width)
        target[layer, own, :] = source[layer, own, :]
        far_target[layer, pl.ds(me, 1)] = far_source[layer, pl.ds(me, 1)]
        target[layer, slots:, :] = jnp.zeros((padded - slots, features), jnp.bfloat16)

    def receive(way, layer):
        target, far_target = ((near_in, far_in), (near_back_in, far_back_in))[way]
        for k in range(span):
            if k != reach:
                near_copy(way, layer, k).wait_recv()

        def wait(step, carry):
            far_arrival(way, layer, step).wait_recv()
            return carry

        lax.fori_loop(1, peers, wait, 0)
        far_rows[...] = far_target[layer].astype(jnp.float32)
        for s in range(cap):
            begin = near_total + s * peers
            for c in range(columns):
                target[layer, begin : begin + peers, c * LANES : (c + 1) * LANES] = far_rows[
                    :, s * columns + c, :
                ].astype(jnp.bfloat16)

    def gathered():
        return dot(pick[...].astype(jnp.bfloat16), states[...])

    def store(i):
        rows = pl.ds(i * BLOCK, BLOCK)
        return pltpu.make_async_copy(edges.at[rows], edge_out.at[rows], store_sems.at[i])

    send(0, 0, gathered(), first=True)

    def renumbered(index):
        value = index.astype(jnp.float32)
        far = value - near_total
        peer = jnp.floor((far + 0.5) * (1.0 / cap))
        return jnp.where(value < near_total, value, near_total + (far - peer * cap) * peers + peer)

    for copy in index_loads:
        copy.wait()
    tiles = edge_count // LANES
    receiver_ids = renumbered(receivers[...])
    spread_rows = lax.broadcasted_iota(jnp.int32, (2 * tiles, LANES), 0)
    lane_ids = lax.broadcasted_iota(jnp.int32, (LANES, LANES), 1).astype(jnp.float32)
    slot_ids = lax.broadcasted_iota(jnp.int32, (hot_t.shape[1], LANES), 0).astype(jnp.float32)
    for side, ids in enumerate((renumbered(senders[...]), receiver_ids)):
        high = 256.0 * jnp.floor(ids * (1.0 / 256.0))
        parts = jnp.transpose(jnp.concatenate([high, ids - high], axis=0)).astype(jnp.bfloat16)
        for b in range(tiles):
            chosen = (spread_rows == b) | (spread_rows == tiles + b)
            column = dot(parts, jnp.where(chosen, 1.0, 0.0).astype(jnp.bfloat16))
            for j in range(padded // LANES):
                begin = side * padded + j * LANES
                hot[b * LANES : (b + 1) * LANES, begin : begin + LANES] = jnp.where(
                    column == lane_ids + j * LANES, 1.0, 0.0
                ).astype(jnp.bfloat16)
    for b in range(tiles):
        begin = (b * LANES) % BLOCK
        hot_t[b * LANES // BLOCK, :, begin : begin + LANES] = jnp.where(
            receiver_ids[b : b + 1] == slot_ids, 1.0, 0.0
        ).astype(jnp.bfloat16)

    def centre(weight, layer):
        values = weight[layer].astype(jnp.float32)
        weight[layer] = (values - jnp.mean(values, axis=-1, keepdims=True)).astype(jnp.bfloat16)

    for copy in own_loads:
        copy.wait()
    for layer in range(layers):

        def own_term(i, carry, layer=layer):
            rows = pl.ds(pl.multiple_of(i * OWN_BLOCK, OWN_BLOCK), OWN_BLOCK)
            partial[rows, :] = 0.5 * (
                dot(edges[rows, :], edge_w1[layer, :features, :]) + edge_b1[layer : layer + 1, :]
            )
            return carry

        if layer == 0:
            lax.fori_loop(0, own_blocks, own_term, 0)
            for copy in late_loads:
                copy.wait()
            centre(edge_w2, 0)

        receive(0, layer)
        arrived = near_in[layer]
        for side in range(2):
            begin = (1 + side) * features
            projected[side * padded : (side + 1) * padded, :] = (
                0.5 * dot(arrived, edge_w1[layer, begin : begin + features, :])
            ).astype(jnp.bfloat16)

        sums[...] = jnp.zeros_like(sums)

        def block_rows(i):
            return pl.ds(i * BLOCK, BLOCK)

        def first_half(i, hidden):
            rows = block_rows(i)
            hidden[...] = gated(partial[rows, :] + dot(hot[rows, :], projected[...]))

        def second_half(i, hidden, layer=layer):
            rows = block_rows(i)
            mixed = dot(hidden[...], edge_w2[layer])
            fresh = edges[rows, :].astype(jnp.float32) + layer_norm(
                mixed, edge_gain[layer : layer + 1, :], edge_shift[layer : layer + 1, :]
            )
            fresh = fresh.astype(jnp.bfloat16)
            edges[rows, :] = fresh
            if layer == layers - 1:
                store(i).start()
            sums[...] += dot(hot_t[i], fresh)

        held = (hidden_even, hidden_odd)
        first_half(0, held[0])
        for i in range(blocks):
            if i + 1 < blocks:
                first_half(i + 1, held[(i + 1) % 2])
            second_half(i, held[i % 2])

        send(1, layer, sums)
        centre(node_w2, layer)
        pre = dot(states[...], node_w1[layer, :features, :]) + node_b1[layer : layer + 1, :]
        if layer + 1 < layers:
            centre(edge_w2, layer + 1)
            lax.fori_loop(0, own_blocks, functools.partial(own_term, layer=layer + 1), 0)
        receive(1, layer)
        aggregate = dot(jnp.transpose(pick[...]).astype(jnp.bfloat16), near_back_in[layer]).astype(jnp.bfloat16)
        half = 0.5 * (pre + dot(aggregate, node_w1[layer, features:, :]))
        mixed = dot(gated(half), node_w2[layer])
        fresh = states[...].astype(jnp.float32) + layer_norm(
            mixed, node_gain[layer : layer + 1, :], node_shift[layer : layer + 1, :]
        )
        states[...] = fresh.astype(jnp.bfloat16)
        if layer + 1 < layers:
            send(0, layer + 1, gathered())

    for i in range(blocks):
        store(i).wait()
    for way in range(2):
        for layer in range(layers):
            for k in range(span):
                if k != reach:
                    near_copy(way, layer, k).wait_send()

            def sent(step, carry, way=way, layer=layer):
                far_copy(way, layer, step).wait_send()
                return carry

            lax.fori_loop(1, peers, sent, 0)


def handed_on(nodes_in, edges_in, nodes_out, edges_out, nodes_held, edges_held, sems):
    pieces = [(nodes_in, nodes_held, nodes_out)]
    for begin in range(0, edges_in.shape[0], BLOCK):
        rows = pl.ds(begin, BLOCK)
        pieces.append((edges_in.at[rows], edges_held.at[rows], edges_out.at[rows]))
    fetches = [pltpu.make_async_copy(a, b, sems.at[0, i]) for i, (a, b, _) in enumerate(pieces)]
    writes = [pltpu.make_async_copy(b, c, sems.at[1, i]) for i, (_, b, c) in enumerate(pieces)]
    for fetch in fetches:
        fetch.start()
    for fetch, write in zip(fetches, writes):
        fetch.wait()
        write.start()
    for write in writes:
        write.wait()


def on_device(
    nodes,
    edges,
    near_table,
    far_table,
    edge_sender,
    edge_receiver,
    edge_w1,
    edge_b1,
    edge_w2,
    edge_gain,
    edge_shift,
    node_w1,
    node_b1,
    node_w2,
    node_gain,
    node_shift,
):
    peers = lax.axis_size(("node", "feat"))
    feat_size = lax.axis_size("feat")
    span, near_width = near_table.shape[1:]
    cap = far_table.shape[2]
    near_total = span * near_width
    near_table = jnp.transpose(near_table, (1, 0, 2))
    far_table = far_table.reshape(peers, cap).T
    slots = near_total + peers * cap
    padded = round_up(slots + 1, LANES)
    node_rows, features = nodes.shape
    edge_count = edges.shape[0]
    layers = edge_w1.shape[0]
    blocks = edge_count // BLOCK
    senders = edge_sender.reshape(edge_count // LANES, LANES)
    receivers = edge_receiver.reshape(edge_count // LANES, LANES)
    tile = cap * features // LANES
    bf16, f32 = jnp.bfloat16, jnp.float32
    sizes = (peers, feat_size, layers, span, near_width, cap, slots)
    vmem = pl.BlockSpec(memory_space=pltpu.VMEM)
    hbm = pl.BlockSpec(memory_space=pltpu.HBM)
    near_buffer = pltpu.VMEM((layers, padded, features), bf16)
    far_buffer = pltpu.VMEM((layers, peers, tile, LANES), bf16)
    flops = 2 * layers * edge_count * features * (2 * features + 2 * padded + slots)
    out_shape = (
        jax.ShapeDtypeStruct(nodes.shape, bf16),
        jax.ShapeDtypeStruct(edges.shape, bf16),
    )
    results = pl.pallas_call(
        functools.partial(kernel, sizes),
        out_shape=out_shape,
        in_specs=[hbm] * 16,
        out_specs=(vmem, hbm),
        scratch_shapes=[
            pltpu.VMEM(edges.shape, bf16),
            pltpu.VMEM(near_table.shape, jnp.int32),
            pltpu.VMEM(far_table.shape, jnp.int32),
            pltpu.VMEM(senders.shape, jnp.int32),
            pltpu.VMEM(receivers.shape, jnp.int32),
        ]
        + [pltpu.VMEM(edge_b1.shape, f32)] * 6
        + [
            pltpu.VMEM(edge_w1.shape, bf16),
            pltpu.VMEM(edge_w2.shape, bf16),
            pltpu.VMEM(node_w1.shape, bf16),
            pltpu.VMEM(node_w2.shape, bf16),
            pltpu.VMEM(edges.shape, f32),
            pltpu.VMEM((BLOCK, features), bf16),
            pltpu.VMEM((BLOCK, features), bf16),
            pltpu.VMEM((edge_count, 2 * padded), bf16),
            pltpu.VMEM((blocks, round_up(slots, 16), BLOCK), bf16),
            pltpu.VMEM((padded, node_rows), f32),
            pltpu.VMEM((2 * padded, features), bf16),
            pltpu.VMEM((round_up(slots, 16), features), f32),
            near_buffer, near_buffer, near_buffer, near_buffer,
            far_buffer, far_buffer, far_buffer, far_buffer,
            pltpu.VMEM((peers, tile, LANES), f32),
            pltpu.SemaphoreType.DMA((15 + layers,)),
            pltpu.SemaphoreType.DMA((blocks,)),
            pltpu.SemaphoreType.DMA((2 * layers * span,)),
            pltpu.SemaphoreType.DMA((2 * layers * span,)),
            pltpu.SemaphoreType.DMA((2 * layers * peers,)),
            pltpu.SemaphoreType.DMA((2 * layers * peers,)),
        ],
        compiler_params=pltpu.CompilerParams(
            collective_id=0, has_side_effects=True, vmem_limit_bytes=62 * 2**20
        ),
        cost_estimate=pl.CostEstimate(flops=flops, bytes_accessed=12 * 2**20, transcendentals=0),
    )(
        nodes, near_table, far_table, senders, receivers,
        edge_b1, edge_gain, edge_shift, node_b1, node_gain, node_shift,
        edges, edge_w1, edge_w2, node_w1, node_w2,
    )
    return pl.pallas_call(
        handed_on,
        out_shape=out_shape,
        in_specs=[hbm] * 2,
        out_specs=(hbm, hbm),
        scratch_shapes=[
            pltpu.VMEM(nodes.shape, bf16),
            pltpu.VMEM(edges.shape, bf16),
            pltpu.SemaphoreType.DMA((2, 1 + blocks)),
        ],
        compiler_params=pltpu.CompilerParams(vmem_limit_bytes=62 * 2**20),
        cost_estimate=pl.CostEstimate(flops=0, bytes_accessed=2 * 2 * (nodes.size + edges.size), transcendentals=0),
    )(*results)


def solution(mesh):
    split = P(AXES, None)
    table = P(AXES, None, None)
    return jax.shard_map(
        on_device,
        mesh=mesh,
        in_specs=(split, split, table, table, P(AXES), P(AXES)) + (P(),) * 10,
        out_specs=(split, split),
        check_vma=False,
    )
```

```python
import functools

import jax
import jax.numpy as jnp
from jax import lax
from jax.experimental import pallas as pl
from jax.experimental.pallas import tpu as pltpu
from jax.sharding import PartitionSpec as P

EPSILON = 1e-05
LANES = 128
BLOCK = 512
OWN_BLOCK = 1024
AXES = ("ens", "node", "feat")
MESH = pl.DeviceIdType.MESH


def round_up(value, multiple):
    return -(-value // multiple) * multiple


def dot(a, b):
    return jnp.dot(a, b, preferred_element_type=jnp.float32)


def layer_norm(center, norm_gain, norm_shift):
    spread = jnp.mean(center * center, axis=-1, keepdims=True)
    return center * lax.rsqrt(spread + EPSILON) * norm_gain + norm_shift


def gated(half):
    return (half + half * jnp.tanh(half)).astype(jnp.bfloat16)


def kernel(
    sizes,
    nodes_hbm, near_hbm, far_hbm, senders_hbm, receivers_hbm,
    edge_b1_hbm, edge_gain_hbm, edge_shift_hbm, node_b1_hbm, node_gain_hbm, node_shift_hbm,
    edges_hbm, edge_w1_hbm, edge_w2_hbm, node_w1_hbm, node_w2_hbm,
    aggregate_out, states_out, pre_out, weight_out, edge_out,
    states, pre, edges,
    near_table, far_table, senders, receivers,
    edge_b1, edge_gain, edge_shift, node_b1, node_gain, node_shift,
    edge_w1, edge_w2, node_w1, node_w2,
    partial, hidden_even, hidden_odd, hot, hot_t, pick, projected, sums,
    near_out, near_in, near_back_out, near_back_in,
    far_out, far_in, far_back_out, far_back_in,
    far_rows,
    load_sems, store_sems, node_sems,
    near_send, near_recv, far_send, far_recv,
):
    peers, feat_size, layers, span, near_width, cap, slots = sizes
    reach = (span - 1) // 2
    near_total = span * near_width
    padded = pick.shape[0]
    features = states.shape[1]
    columns = features // LANES
    edge_count = edges.shape[0]
    blocks = edge_count // BLOCK
    own_blocks = edge_count // OWN_BLOCK
    ens = lax.axis_index("ens")
    me = lax.axis_index("node") * feat_size + lax.axis_index("feat")

    def device(index):
        return (ens, lax.div(index, feat_size), lax.rem(index, feat_size))

    def around(index):
        return jnp.where(index >= peers, index - peers, index)

    loads = []

    def load(source, target):
        copy = pltpu.make_async_copy(source, target, load_sems.at[len(loads)])
        copy.start()
        loads.append(copy)
        return copy

    first_loads = [load(nodes_hbm, states), load(near_hbm, near_table), load(far_hbm, far_table)]
    index_loads = [load(senders_hbm, senders), load(receivers_hbm, receivers)]
    own_loads = [load(edge_b1_hbm, edge_b1), load(edges_hbm, edges), load(edge_w1_hbm.at[0], edge_w1.at[0])]
    late_loads = [
        load(edge_gain_hbm, edge_gain),
        load(edge_shift_hbm, edge_shift),
        load(node_b1_hbm, node_b1),
        load(node_gain_hbm, node_gain),
        load(node_shift_hbm, node_shift),
        load(edge_w2_hbm, edge_w2),
        load(node_w1_hbm, node_w1),
        load(node_w2_hbm, node_w2),
    ]
    late_loads += [load(edge_w1_hbm.at[layer], edge_w1.at[layer]) for layer in range(1, layers)]

    barrier = pltpu.get_barrier_semaphore()

    def greet(step, carry):
        pl.semaphore_signal(barrier, inc=1, device_id=device(around(me + step)), device_id_type=MESH)
        return carry

    lax.fori_loop(1, peers, greet, 0)

    for copy in first_loads:
        copy.wait()
    node_rows = states.shape[0]
    near_ids = lax.broadcasted_iota(jnp.int32, (near_width, node_rows), 1).astype(jnp.float32)
    far_ids = lax.broadcasted_iota(jnp.int32, (peers, node_rows), 1).astype(jnp.float32)
    for k in range(span):
        row = near_table[k].astype(jnp.float32)
        column = jnp.transpose(jnp.broadcast_to(row, (node_rows, near_width)))
        pick[k * near_width : (k + 1) * near_width, :] = jnp.where(column == near_ids, 1.0, 0.0)
    for s in range(cap):
        begin = near_total + s * peers
        row = far_table[s : s + 1, :].astype(jnp.float32)
        column = jnp.transpose(jnp.broadcast_to(row, (node_rows, peers)))
        pick[begin : begin + peers, :] = jnp.where(column == far_ids, 1.0, 0.0)
    pick[slots:, :] = jnp.zeros((padded - slots, node_rows), jnp.float32)

    def near_copy(way, layer, k):
        source, target = ((near_out, near_in), (near_back_out, near_back_in))[way]
        rows = pl.ds(k * near_width, near_width)
        shift = (k - reach) if way == 0 else (reach - k)
        slot = (way * layers + layer) * span + k
        return pltpu.make_async_remote_copy(
            src_ref=source.at[layer, rows],
            dst_ref=target.at[layer, rows],
            send_sem=near_send.at[slot],
            recv_sem=near_recv.at[slot],
            device_id=device(around(me + (shift + peers) % peers)),
            device_id_type=MESH,
        )

    def far_copy(way, layer, step):
        source, target = ((far_out, far_in), (far_back_out, far_back_in))[way]
        to = around(me + step)
        slot = (way * layers + layer) * peers + step
        return pltpu.make_async_remote_copy(
            src_ref=source.at[layer, to],
            dst_ref=target.at[layer, me],
            send_sem=far_send.at[slot],
            recv_sem=far_recv.at[slot],
            device_id=device(to),
            device_id_type=MESH,
        )

    def far_arrival(way, layer, step):
        source, target = ((far_out, far_in), (far_back_out, far_back_in))[way]
        origin = around(me + peers - step)
        slot = (way * layers + layer) * peers + step
        return pltpu.make_async_remote_copy(
            src_ref=source.at[layer, origin],
            dst_ref=target.at[layer, origin],
            send_sem=far_send.at[slot],
            recv_sem=far_recv.at[slot],
            device_id=device(origin),
            device_id_type=MESH,
        )

    def send(way, layer, rows, first=False):
        source, far_source = ((near_out, far_out), (near_back_out, far_back_out))[way]
        target, far_target = ((near_in, far_in), (near_back_in, far_back_in))[way]
        source[layer, :near_total, :] = rows[:near_total].astype(jnp.bfloat16)
        if first:
            pl.semaphore_wait(barrier, peers - 1)
        for k in range(span):
            if k != reach:
                near_copy(way, layer, k).start()
        for s in range(cap):
            begin = near_total + s * peers
            for c in range(columns):
                far_rows[:, s * columns + c, :] = rows[begin : begin + peers, c * LANES : (c + 1) * LANES]
        far_source[layer] = far_rows[...].astype(jnp.bfloat16)

        def start(step, carry):
            far_copy(way, layer, step).start()
            return carry

        lax.fori_loop(1, peers, start, 0)
        own = slice(reach * near_width, (reach + 1) * near_width)
        target[layer, own, :] = source[layer, own, :]
        far_target[layer, pl.ds(me, 1)] = far_source[layer, pl.ds(me, 1)]
        target[layer, slots:, :] = jnp.zeros((padded - slots, features), jnp.bfloat16)

    def receive(way, layer):
        target, far_target = ((near_in, far_in), (near_back_in, far_back_in))[way]

        def sent(step, carry):
            far_copy(way, layer, step).wait_send()
            return carry

        lax.fori_loop(1, peers, sent, 0)
        for k in range(span):
            if k != reach:
                near_copy(way, layer, k).wait_send()
        for k in range(span):
            if k != reach:
                near_copy(way, layer, k).wait_recv()

        def wait(step, carry):
            far_arrival(way, layer, step).wait_recv()
            return carry

        lax.fori_loop(1, peers, wait, 0)
        far_rows[...] = far_target[layer].astype(jnp.float32)
        for s in range(cap):
            begin = near_total + s * peers
            for c in range(columns):
                target[layer, begin : begin + peers, c * LANES : (c + 1) * LANES] = far_rows[
                    :, s * columns + c, :
                ].astype(jnp.bfloat16)

    def gathered():
        return dot(pick[...].astype(jnp.bfloat16), states[...])

    def store(i):
        rows = pl.ds(i * BLOCK, BLOCK)
        return pltpu.make_async_copy(edges.at[rows], edge_out.at[rows], store_sems.at[i])

    send(0, 0, gathered(), first=True)

    def renumbered(index):
        value = index.astype(jnp.float32)
        far = value - near_total
        peer = jnp.floor((far + 0.5) * (1.0 / cap))
        return jnp.where(value < near_total, value, near_total + (far - peer * cap) * peers + peer)

    for copy in index_loads:
        copy.wait()
    tiles = edge_count // LANES
    receiver_ids = renumbered(receivers[...])
    spread_rows = lax.broadcasted_iota(jnp.int32, (2 * tiles, LANES), 0)
    lane_ids = lax.broadcasted_iota(jnp.int32, (LANES, LANES), 1).astype(jnp.float32)
    slot_ids = lax.broadcasted_iota(jnp.int32, (hot_t.shape[1], LANES), 0).astype(jnp.float32)
    for side, ids in enumerate((renumbered(senders[...]), receiver_ids)):
        high = 256.0 * jnp.floor(ids * (1.0 / 256.0))
        parts = jnp.transpose(jnp.concatenate([high, ids - high], axis=0)).astype(jnp.bfloat16)
        for b in range(tiles):
            chosen = (spread_rows == b) | (spread_rows == tiles + b)
            column = dot(parts, jnp.where(chosen, 1.0, 0.0).astype(jnp.bfloat16))
            for j in range(padded // LANES):
                begin = side * padded + j * LANES
                hot[b * LANES : (b + 1) * LANES, begin : begin + LANES] = jnp.where(
                    column == lane_ids + j * LANES, 1.0, 0.0
                ).astype(jnp.bfloat16)
    for b in range(tiles):
        begin = (b * LANES) % BLOCK
        hot_t[b * LANES // BLOCK, :, begin : begin + LANES] = jnp.where(
            receiver_ids[b : b + 1] == slot_ids, 1.0, 0.0
        ).astype(jnp.bfloat16)

    def centre(weight, layer):
        values = weight[layer].astype(jnp.float32)
        weight[layer] = (values - jnp.mean(values, axis=-1, keepdims=True)).astype(jnp.bfloat16)

    for copy in own_loads:
        copy.wait()
    for layer in range(layers):

        def own_term(i, carry, layer=layer):
            rows = pl.ds(pl.multiple_of(i * OWN_BLOCK, OWN_BLOCK), OWN_BLOCK)
            partial[rows, :] = 0.5 * (
                dot(edges[rows, :], edge_w1[layer, :features, :]) + edge_b1[layer : layer + 1, :]
            )
            return carry

        if layer == 0:
            lax.fori_loop(0, own_blocks, own_term, 0)
            for copy in late_loads:
                copy.wait()
            centre(edge_w2, 0)

        receive(0, layer)
        arrived = near_in[layer]
        for side in range(2):
            begin = (1 + side) * features
            projected[side * padded : (side + 1) * padded, :] = (
                0.5 * dot(arrived, edge_w1[layer, begin : begin + features, :])
            ).astype(jnp.bfloat16)

        sums[...] = jnp.zeros_like(sums)

        def block_rows(i):
            return pl.ds(i * BLOCK, BLOCK)

        def first_half(i, hidden):
            rows = block_rows(i)
            hidden[...] = gated(partial[rows, :] + dot(hot[rows, :], projected[...]))

        def second_half(i, hidden, layer=layer):
            rows = block_rows(i)
            mixed = dot(hidden[...], edge_w2[layer])
            fresh = edges[rows, :].astype(jnp.float32) + layer_norm(
                mixed, edge_gain[layer : layer + 1, :], edge_shift[layer : layer + 1, :]
            )
            fresh = fresh.astype(jnp.bfloat16)
            edges[rows, :] = fresh
            if layer == layers - 1:
                store(i).start()
            sums[...] += dot(hot_t[i], fresh)

        held = (hidden_even, hidden_odd)
        first_half(0, held[0])
        for i in range(blocks):
            if i + 1 < blocks:
                first_half(i + 1, held[(i + 1) % 2])
            second_half(i, held[i % 2])

        send(1, layer, sums)
        centre(node_w2, layer)
        pre[...] = dot(states[...], node_w1[layer, :features, :]) + node_b1[layer : layer + 1, :]
        if layer == layers - 1:
            node_stores = [
                pltpu.make_async_copy(states, states_out, node_sems.at[0]),
                pltpu.make_async_copy(pre, pre_out, node_sems.at[1]),
                pltpu.make_async_copy(node_w2.at[layer], weight_out, node_sems.at[2]),
            ]
            for copy in node_stores:
                copy.start()
        if layer + 1 < layers:
            centre(edge_w2, layer + 1)
            lax.fori_loop(0, own_blocks, functools.partial(own_term, layer=layer + 1), 0)
        receive(1, layer)
        aggregate = dot(jnp.transpose(pick[...]).astype(jnp.bfloat16), near_back_in[layer]).astype(jnp.bfloat16)
        if layer == layers - 1:
            aggregate_out[...] = aggregate
            break
        half = 0.5 * (pre[...] + dot(aggregate, node_w1[layer, features:, :]))
        mixed = dot(gated(half), node_w2[layer])
        fresh = states[...].astype(jnp.float32) + layer_norm(
            mixed, node_gain[layer : layer + 1, :], node_shift[layer : layer + 1, :]
        )
        states[...] = fresh.astype(jnp.bfloat16)
        send(0, layer + 1, gathered())

    for copy in node_stores:
        copy.wait()
    for i in range(blocks):
        store(i).wait()


def last_step(
    aggregate_hbm, states_hbm, pre_hbm, weight_hbm, node_w1_hbm, gain_hbm, shift_hbm, edges_hbm,
    node_out, edge_out,
    aggregate, states, pre, second, first, gain, shift, edges,
    sems, fetch_sems, write_sems,
):
    layer = gain.shape[0] - 1
    features = states.shape[1]
    loads = [
        pltpu.make_async_copy(source, target, sems.at[i])
        for i, (source, target) in enumerate(
            (
                (aggregate_hbm, aggregate),
                (node_w1_hbm.at[layer, pl.ds(features, features)], first),
                (pre_hbm, pre),
                (weight_hbm, second),
                (states_hbm, states),
                (gain_hbm, gain),
                (shift_hbm, shift),
            )
        )
    ]
    fetches, writes = [], []
    for i in range(edges.shape[0] // LANES):
        rows = pl.ds(i * LANES, LANES)
        fetches.append(pltpu.make_async_copy(edges_hbm.at[rows], edges.at[rows], fetch_sems.at[i]))
        writes.append(pltpu.make_async_copy(edges.at[rows], edge_out.at[rows], write_sems.at[i]))
    for copy in loads + fetches:
        copy.start()
    for copy in loads:
        copy.wait()
    middle = len(fetches) // 2
    for fetch, write in zip(fetches[:middle], writes[:middle]):
        fetch.wait()
        write.start()
    half = 0.5 * (pre[...] + dot(aggregate[...], first[...]))
    mixed = dot(gated(half), second[...])
    for fetch, write in zip(fetches[middle:], writes[middle:]):
        fetch.wait()
        write.start()
    fresh = states[...].astype(jnp.float32) + layer_norm(
        mixed, gain[layer : layer + 1, :], shift[layer : layer + 1, :]
    )
    node_out[...] = fresh.astype(jnp.bfloat16)
    for write in writes:
        write.wait()


def on_device(
    nodes,
    edges,
    near_table,
    far_table,
    edge_sender,
    edge_receiver,
    edge_w1,
    edge_b1,
    edge_w2,
    edge_gain,
    edge_shift,
    node_w1,
    node_b1,
    node_w2,
    node_gain,
    node_shift,
):
    peers = lax.axis_size(("node", "feat"))
    feat_size = lax.axis_size("feat")
    span, near_width = near_table.shape[1:]
    cap = far_table.shape[2]
    near_total = span * near_width
    near_table = jnp.transpose(near_table, (1, 0, 2))
    far_table = far_table.reshape(peers, cap).T
    slots = near_total + peers * cap
    padded = round_up(slots + 1, LANES)
    node_rows, features = nodes.shape
    edge_count = edges.shape[0]
    layers = edge_w1.shape[0]
    blocks = edge_count // BLOCK
    senders = edge_sender.reshape(edge_count // LANES, LANES)
    receivers = edge_receiver.reshape(edge_count // LANES, LANES)
    tile = cap * features // LANES
    bf16, f32 = jnp.bfloat16, jnp.float32
    sizes = (peers, feat_size, layers, span, near_width, cap, slots)
    vmem = pl.BlockSpec(memory_space=pltpu.VMEM)
    hbm = pl.BlockSpec(memory_space=pltpu.HBM)
    near_buffer = pltpu.VMEM((layers, padded, features), bf16)
    far_buffer = pltpu.VMEM((layers, peers, tile, LANES), bf16)
    flops = 2 * layers * edge_count * features * (2 * features + 2 * padded + slots)
    out_shape = (
        jax.ShapeDtypeStruct(nodes.shape, bf16),
        jax.ShapeDtypeStruct(edges.shape, bf16),
    )
    aggregate, states, pre, weight, edge_state = pl.pallas_call(
        functools.partial(kernel, sizes),
        out_shape=(
            out_shape[0],
            out_shape[0],
            jax.ShapeDtypeStruct(nodes.shape, f32),
            jax.ShapeDtypeStruct(node_w2.shape[1:], bf16),
            out_shape[1],
        ),
        in_specs=[hbm] * 16,
        out_specs=(vmem, hbm, hbm, hbm, hbm),
        scratch_shapes=[
            pltpu.VMEM(nodes.shape, bf16),
            pltpu.VMEM(nodes.shape, f32),
            pltpu.VMEM(edges.shape, bf16),
            pltpu.VMEM(near_table.shape, jnp.int32),
            pltpu.VMEM(far_table.shape, jnp.int32),
            pltpu.VMEM(senders.shape, jnp.int32),
            pltpu.VMEM(receivers.shape, jnp.int32),
        ]
        + [pltpu.VMEM(edge_b1.shape, f32)] * 6
        + [
            pltpu.VMEM(edge_w1.shape, bf16),
            pltpu.VMEM(edge_w2.shape, bf16),
            pltpu.VMEM(node_w1.shape, bf16),
            pltpu.VMEM(node_w2.shape, bf16),
            pltpu.VMEM(edges.shape, f32),
            pltpu.VMEM((BLOCK, features), bf16),
            pltpu.VMEM((BLOCK, features), bf16),
            pltpu.VMEM((edge_count, 2 * padded), bf16),
            pltpu.VMEM((blocks, round_up(slots, 16), BLOCK), bf16),
            pltpu.VMEM((padded, node_rows), f32),
            pltpu.VMEM((2 * padded, features), bf16),
            pltpu.VMEM((round_up(slots, 16), features), f32),
            near_buffer, near_buffer, near_buffer, near_buffer,
            far_buffer, far_buffer, far_buffer, far_buffer,
            pltpu.VMEM((peers, tile, LANES), f32),
            pltpu.SemaphoreType.DMA((15 + layers,)),
            pltpu.SemaphoreType.DMA((blocks,)),
            pltpu.SemaphoreType.DMA((3,)),
            pltpu.SemaphoreType.DMA((2 * layers * span,)),
            pltpu.SemaphoreType.DMA((2 * layers * span,)),
            pltpu.SemaphoreType.DMA((2 * layers * peers,)),
            pltpu.SemaphoreType.DMA((2 * layers * peers,)),
        ],
        compiler_params=pltpu.CompilerParams(
            collective_id=0, has_side_effects=True, vmem_limit_bytes=62 * 2**20
        ),
        cost_estimate=pl.CostEstimate(flops=flops, bytes_accessed=12 * 2**20, transcendentals=0),
    )(
        nodes, near_table, far_table, senders, receivers,
        edge_b1, edge_gain, edge_shift, node_b1, node_gain, node_shift,
        edges, edge_w1, edge_w2, node_w1, node_w2,
    )
    return pl.pallas_call(
        last_step,
        out_shape=out_shape,
        in_specs=[hbm] * 8,
        out_specs=(vmem, hbm),
        scratch_shapes=[
            pltpu.VMEM(nodes.shape, bf16),
            pltpu.VMEM(nodes.shape, bf16),
            pltpu.VMEM(nodes.shape, f32),
            pltpu.VMEM(node_w2.shape[1:], bf16),
            pltpu.VMEM(node_w2.shape[1:], bf16),
            pltpu.VMEM(node_gain.shape, f32),
            pltpu.VMEM(node_shift.shape, f32),
            pltpu.VMEM(edges.shape, bf16),
            pltpu.SemaphoreType.DMA((7,)),
            pltpu.SemaphoreType.DMA((edge_count // LANES,)),
            pltpu.SemaphoreType.DMA((edge_count // LANES,)),
        ],
        compiler_params=pltpu.CompilerParams(vmem_limit_bytes=62 * 2**20),
        cost_estimate=pl.CostEstimate(flops=0, bytes_accessed=2 * 2 * (nodes.size + edges.size), transcendentals=0),
    )(aggregate, states, pre, weight, node_w1, node_gain, node_shift, edge_state)


def solution(mesh):
    split = P(AXES, None)
    table = P(AXES, None, None)
    return jax.shard_map(
        on_device,
        mesh=mesh,
        in_specs=(split, split, table, table, P(AXES), P(AXES)) + (P(),) * 10,
        out_specs=(split, split),
        check_vma=False,
    )
```
